768 devices in a mesh: gx: 24 (over z, core), gy: 8 (over y), gz: 4 (over x).
Axes of the slice: x: 4, y: 8, z: 12, core: 2. Of those that a mesh axis runs over, the one named last changes fastest.
Arguments:
- operator: bfloat16 [24, 8, 3072, 3072], P('gx', 'gy', 'gz'), may hold values from -1 to 4
- rhs_parts: float32 [24, 8, 8, 3072], P('gx', 'gy'), may hold values from -6 to 6
- stiffness: float32 [24, 8, 3072], P('gx', 'gy'), may hold values from 1 to 10
- traces: float32 [24, 8, 6, 3072], P('gx', 'gy'), may hold values from -6 to 6
- coarse_inverse: float32 [24, 8, 6, 1152], P('gx', 'gy'), may hold values from -1 to 1, as said below
- rigid_loads: float32 [24, 8, 6, 8], P('gx', 'gy'), may hold values from -8192 to 8192
- face_lengths: int32 [24, 8, 4], P('gx', 'gy'), may hold values from 0 to 768, as said below
- face_order: int32 [24, 8, 4, 768], P('gx', 'gy'), may hold values from 0 to 767, as said below
- mode_count: int32 [24, 8], P('gx', 'gy'), may hold values from 0 to 6, as said below
Outputs:
- multipliers: float32 [24, 8, 8, 3072], P('gx', 'gy')
The draws below stay inside these ranges and needn't reach their ends.
Inputs may be any that keep to these rules, and one draw needn't show every extreme that they name: `coarse_inverse`: symmetric over the coefficient ordering. `face_lengths`: a face on the grid's edge has length 0; the two sides of an interface have the same length. `face_order`: on each face the live slots map one to one onto the neighbour's live slots of the opposite face, and that face maps them back; other slots map to themselves. `mode_count`: subdomains off the grid's edge have 6.
All inputs are finite; a program needn't handle non-finite values.
Results may differ from the reference program's by a relative error of at most 0.0036.
Values may be sent and summed in bfloat16 or wider, within the bound.
A program may use at most 32 MiB of HBM per device.

```python
import math
import jax
import jax.numpy as jnp
from jax import lax

ORDER = 3072
LOADS = 8
MODES = 6
ITERS = 2
CAP = 768
SX = 24
SY = 8
COARSE = 1152


def side_order(key, lengths):
    position = lax.broadcasted_iota(jnp.int32, (SX, SY, CAP), 2)
    scores = jax.random.randint(key, (SX, SY, CAP), 0, 2 ** 19) * CAP + position
    scores = jnp.where(position < lengths[:, :, None], scores, 2 ** 30 + position)
    return jnp.argsort(scores, axis=-1).astype(jnp.int32)


def interfaces(key):
    first_index = lax.broadcasted_iota(jnp.int32, (SX, SY), 0)
    second_index = lax.broadcasted_iota(jnp.int32, (SX, SY), 1)
    east_len = CAP - jax.random.randint(jax.random.fold_in(key, 11), (SX, SY), 0, CAP // 2 + 1)
    east_len = jnp.where((first_index == 0) & (second_index == 0), CAP, east_len)
    east_len = jnp.where(first_index == SX - 1, 0, east_len)
    north_len = CAP - jax.random.randint(jax.random.fold_in(key, 12), (SX, SY), 0, CAP // 2 + 1)
    north_len = jnp.where(second_index == SY - 1, 0, north_len)
    east_order = side_order(jax.random.fold_in(key, 13), east_len)
    north_order = side_order(jax.random.fold_in(key, 14), north_len)
    east_back = jnp.argsort(east_order, axis=-1).astype(jnp.int32)
    north_back = jnp.argsort(north_order, axis=-1).astype(jnp.int32)
    identity = lax.broadcasted_iota(jnp.int32, (SX, SY, CAP), 2)
    west_order = jnp.concatenate([identity[:1], east_back[:-1]], axis=0)
    south_order = jnp.concatenate([identity[:, :1], north_back[:, :-1]], axis=1)
    west_len = jnp.concatenate([jnp.zeros((1, SY), jnp.int32), east_len[:-1]], axis=0)
    south_len = jnp.concatenate([jnp.zeros((SX, 1), jnp.int32), north_len[:, :-1]], axis=1)
    lengths = jnp.stack([west_len, east_len, south_len, north_len], axis=-1).astype(jnp.int32)
    orders = jnp.stack([west_order, east_order, south_order, north_order], axis=2).astype(jnp.int32)
    return (lengths, orders)


def draw_face_lengths(key, part):
    return interfaces(key)[0]


def draw_face_order(key, part):
    return interfaces(key)[1]


def draw_mode_count(key, part):
    key = jax.random.fold_in(key, 21)
    first_index = lax.broadcasted_iota(jnp.int32, (SX, SY), 0)
    second_index = lax.broadcasted_iota(jnp.int32, (SX, SY), 1)
    inner = (first_index > 0) & (first_index < SX - 1) & (second_index > 0) & (second_index < SY - 1)
    edge_count = jax.random.randint(key, (SX, SY), 0, MODES + 1)
    return jnp.where(inner, MODES, edge_count).astype(jnp.int32)


def draw_operator(key, part):
    key = jax.random.fold_in(key, 31)
    noise_key = jax.random.fold_in(key, 1)
    diag_key = jax.random.fold_in(key, 2)
    shape = (SX, SY, ORDER, ORDER)
    noise = jnp.clip(jax.random.normal(noise_key, shape, jnp.float32), -4.0, 4.0)
    diagonal = jax.random.uniform(diag_key, (SX, SY, ORDER, 1), jnp.float32, 1.0, 2.0)
    row_index = lax.broadcasted_iota(jnp.int32, shape, 2)
    column_index = lax.broadcasted_iota(jnp.int32, shape, 3)
    values = 0.25 / ORDER ** 0.5 * noise + 0.5 / ORDER + jnp.where(row_index == column_index, diagonal, 0.0)
    return values.astype(jnp.bfloat16)


def draw_traces(key, part):
    key = jax.random.fold_in(key, 41)
    noise_key = jax.random.fold_in(key, 1)
    offset_key = jax.random.fold_in(key, 2)
    shape = (SX, SY, MODES, ORDER)
    noise = jnp.clip(jax.random.normal(noise_key, shape, jnp.float32), -4.0, 4.0)
    offset = jax.random.uniform(offset_key, (SX, SY, MODES, 1), jnp.float32, -1.0, 1.0)
    return noise + offset


def draw_rhs_parts(key, part):
    key = jax.random.fold_in(key, 51)
    noise_key = jax.random.fold_in(key, 1)
    offset_key = jax.random.fold_in(key, 2)
    shape = (SX, SY, LOADS, ORDER)
    noise = jnp.clip(jax.random.normal(noise_key, shape, jnp.float32), -4.0, 4.0)
    offset = jax.random.uniform(offset_key, (SX, SY, LOADS, 1), jnp.float32, -1.5, 1.5)
    return noise + offset


def draw_coarse_inverse(key, part):
    key = jax.random.fold_in(key, 61)
    noise_key = jax.random.fold_in(key, 1)
    gain_key = jax.random.fold_in(key, 2)
    shape = (COARSE, COARSE)
    noise = jnp.clip(jax.random.normal(noise_key, shape, jnp.float32), -4.0, 4.0)
    gain = jax.random.uniform(gain_key, (COARSE, 1), jnp.float32, 0.5, 1.0)
    symmetric = (noise + noise.T) * (0.15 / (2.0 * COARSE) ** 0.5)
    row_index = lax.broadcasted_iota(jnp.int32, shape, 0)
    column_index = lax.broadcasted_iota(jnp.int32, shape, 1)
    values = (symmetric + jnp.where(row_index == column_index, gain, 0.0)) / ORDER
    return values.reshape(SX, SY, MODES, COARSE)


def block_scale(rng, extent, pieces, least, top_value):
    def one(axis_at, blocks):
        draws = jax.random.uniform(jax.random.fold_in(jax.random.fold_in(rng, 6), axis_at), (blocks,), jnp.float32, least / len(pieces), top_value / len(pieces))
        return jnp.repeat(jnp.exp(draws), extent[axis_at] // blocks).reshape((-1,) + (1,) * (len(extent) - axis_at - 1))

    level = one(*pieces[0])
    for cut in pieces[1:]:
        level = level * one(*cut)
    return level


def gaussian(key, dims, spread, most, pieces=(), kind=jnp.bfloat16):
    entries = jax.random.normal(key, dims, jnp.float32) * spread
    if len(pieces) > 0:
        entries = block_scale(key, dims, pieces, -0.22, 0.18) * entries
    return jnp.clip(entries, min=-most, max=most).astype(kind)


def setup_inputs(seed: int = 0) -> dict:
    key_of = jax.random.split(jax.random.key(seed), 10)
    return {
        "operator": draw_operator(jax.random.fold_in(key_of[9], 71), 0),
        "rhs_parts": draw_rhs_parts(jax.random.fold_in(key_of[9], 71), 0),
        "stiffness": jnp.clip(jnp.exp(math.log(10.0) - 2.3025851 * jax.random.uniform(key_of[2], (SX, SY, ORDER), jnp.float32) ** block_scale(key_of[2], (SX, SY, ORDER), ((0, 24), (1, 8)), -0.2, 0.2)), 1.0, 10.0),
        "traces": draw_traces(jax.random.fold_in(key_of[9], 71), 0),
        "coarse_inverse": draw_coarse_inverse(jax.random.fold_in(key_of[9], 71), 0),
        "rigid_loads": gaussian(key_of[5], (SX, SY, MODES, LOADS), (ORDER / 2), 8192.0, ((0, 24), (1, 8)), jnp.float32),
        "face_lengths": draw_face_lengths(jax.random.fold_in(key_of[9], 71), 0),
        "face_order": draw_face_order(jax.random.fold_in(key_of[9], 71), 0),
        "mode_count": draw_mode_count(jax.random.fold_in(key_of[9], 71), 0),
    }


highest = lax.Precision.HIGHEST


def reference(operator, rhs_parts, stiffness, traces, coarse_inverse, rigid_loads, face_lengths, face_order, mode_count):
    position = jnp.arange(ORDER) % CAP
    face_index = jnp.arange(ORDER) // CAP
    live_mask = (position[None, None, :] < face_lengths[:, :, face_index]).astype(jnp.float32)
    mode_mask = (jnp.arange(MODES)[None, None, :] < mode_count[:, :, None]).astype(jnp.float32)
    active_modes = traces * mode_mask[:, :, :, None]

    def partner(vectors):
        row_count = vectors.shape[2]
        blocks = vectors.reshape(SX, SY, row_count, 4, CAP)
        edge_x = jnp.zeros((1, SY, row_count, CAP), jnp.float32)
        edge_y = jnp.zeros((SX, 1, row_count, CAP), jnp.float32)
        from_west = jnp.concatenate([edge_x, blocks[:-1, :, :, 1]], axis=0)
        from_east = jnp.concatenate([blocks[1:, :, :, 0], edge_x], axis=0)
        from_south = jnp.concatenate([edge_y, blocks[:, :-1, :, 3]], axis=1)
        from_north = jnp.concatenate([blocks[:, 1:, :, 2], edge_y], axis=1)
        facing = jnp.stack([from_west, from_east, from_south, from_north], axis=3)
        partner_slots = jnp.broadcast_to(face_order[:, :, None], facing.shape)
        return jnp.take_along_axis(facing, partner_slots, axis=4).reshape(SX, SY, row_count, ORDER)

    def assemble(vectors):
        return live_mask[:, :, None] * (vectors + partner(vectors))

    def coarse_solve(coarse_rhs):
        stacked = coarse_rhs.reshape(COARSE, LOADS)
        solved = jnp.dot(coarse_inverse.reshape(COARSE, COARSE), stacked, precision=highest)
        return solved.reshape(SX, SY, MODES, LOADS)

    def correction(coeffs):
        return assemble(jnp.einsum("xyml,xymi->xyli", coeffs, active_modes, precision=highest))

    def project(vectors):
        coarse_rhs = jnp.einsum("xymi,xyli->xyml", active_modes, vectors, precision=highest)
        return vectors - correction(coarse_solve(coarse_rhs))

    def apply_operator(vectors):
        matrices = operator.reshape(SX * SY, ORDER, ORDER)
        inputs = vectors.astype(jnp.bfloat16).reshape(SX * SY, LOADS, ORDER)

        def single(operands):
            return jnp.dot(operands[1], operands[0].T, preferred_element_type=jnp.float32).astype(jnp.bfloat16)

        return lax.map(single, (matrices, inputs)).reshape(SX, SY, LOADS, ORDER)

    estimate = correction(coarse_solve(rigid_loads * mode_mask[:, :, :, None]))
    stiff_sum = assemble(stiffness[:, :, None, :])[:, :, 0]
    weight = live_mask / (stiff_sum + 1.0 - live_mask)
    residual = project(assemble(rhs_parts - apply_operator(estimate).astype(jnp.float32)))
    direction = residual
    previous = jnp.ones((LOADS,), jnp.float32)
    for iteration in range(ITERS):
        scaled = weight[:, :, None] * residual
        resid_dot = jnp.sum(residual * scaled, axis=(0, 1, 3))
        projected = project(scaled)
        if iteration == 0:
            direction = projected
        else:
            direction = projected + (resid_dot / previous)[None, None, :, None] * direction
        image = assemble(apply_operator(direction).astype(jnp.float32))
        curvature = jnp.sum(direction * image, axis=(0, 1, 3))
        step_size = resid_dot / curvature
        estimate = estimate + step_size[None, None, :, None] * direction
        if iteration + 1 < ITERS:
            residual = residual - step_size[None, None, :, None] * project(image)
        previous = resid_dot
    return estimate
```

```python
import functools

import jax
import jax.numpy as jnp
from jax import lax
from jax.experimental import pallas as pl
from jax.experimental.pallas import tpu as pltpu
from jax.sharding import PartitionSpec as P

MESH = pl.DeviceIdType.MESH
GATHERS = 6
PRODUCTS = 2
LANES = 128


def kernel(
    sizes,
    op_ref,
    rhs_ref,
    stiff_ref,
    traces_ref,
    inverse_ref,
    loads_ref,
    lengths_ref,
    order_ref,
    count_ref,
    out_ref,
    op_v,
    faces_out,
    faces_in,
    rows_pad,
    coarse,
    plane,
    column,
    peers,
    blocks,
    lo_ref,
    hi_ref,
    own_e,
    near_e,
    weight,
    known,
    resid,
    direct,
    image,
    op_sem,
    setup_send,
    setup_recv,
    coarse_send,
    coarse_recv,
    plane_send,
    plane_recv,
    column_send,
    column_recv,
    peer_send,
    peer_recv,
    block_send,
    block_recv,
):
    nx, ny, nz = sizes
    cap = order_ref.shape[1]
    order = rhs_ref.shape[1]
    tiles = cap // LANES
    modes = traces_ref.shape[0]
    chips = nx // 2
    plane_size = 2 * ny
    spread = plane_size * modes
    gx, gy, gz = lax.axis_index("gx"), lax.axis_index("gy"), lax.axis_index("gz")
    chip, core = gx // 2, gx % 2

    def near(face, z):
        sign = 2 * (face % 2) - 1
        along_x = 1 - face // 2
        return (
            lax.rem(gx + along_x * sign + nx, nx),
            lax.rem(gy + (1 - along_x) * sign + ny, ny),
            z,
        )

    def opposite(face):
        return face + 1 - 2 * (face % 2)

    peer_list = [(gx, gy, lax.rem(gz + k, nz)) for k in range(1, nz)]
    plane_list = [
        (chip * 2 + lax.rem(core + c, 2), lax.rem(gy + k, ny), gz)
        for c in range(2)
        for k in range(ny)
        if c or k
    ]
    column_list = [(lax.rem(gx + 2 * k, nx), gy, gz) for k in range(1, chips)]
    face_list = [near(f, gz) for f in range(4)]
    product_list = [near(gz, k) for k in range(nz)]
    source_list = [near(f, opposite(f)) for f in range(4)]

    op_copy = pltpu.make_async_copy(op_ref, op_v, op_sem)
    op_copy.start()

    barrier = pltpu.get_barrier_semaphore()
    greeted = peer_list + plane_list + column_list + face_list + source_list
    for target in greeted:
        pl.semaphore_signal(barrier, inc=1, device_id=target, device_id_type=MESH)

    sub = lax.broadcasted_iota(jnp.int32, (8, LANES), 0)
    lane = lax.broadcasted_iota(jnp.int32, (8, LANES), 1)

    def send(src, dst, send_sem, recv_sem, target):
        pltpu.make_async_remote_copy(
            src_ref=src,
            dst_ref=dst,
            send_sem=send_sem,
            recv_sem=recv_sem,
            device_id=target,
            device_id_type=MESH,
        ).start()

    def await_bytes(ref, sem):
        pltpu.make_async_copy(ref, ref, sem).wait()

    def take(values, index):
        return jnp.take_along_axis(values, index, axis=1, mode="promise_in_bounds")

    def row_of(columns):
        total = jnp.zeros((8, LANES), jnp.float32)
        for m, value in columns:
            total = total + jnp.where(lane == 8 * m + sub, value, 0.0)
        return jnp.sum(total, axis=0, keepdims=True)

    pick = jnp.where(lane < spread, 8 * (lane % modes) + sub, 8 * modes + sub)
    my_slot = core * ny + gy

    def gather_start(g, row):
        plane[g, pl.ds(my_slot, 1), :] = row
        mine = plane.at[g, pl.ds(my_slot, 1)]
        for target in plane_list:
            send(mine, mine, plane_send.at[g], plane_recv.at[g], target)

    def gather_finish(g):
        await_bytes(plane.at[g, pl.ds(0, plane_size - 1)], plane_recv.at[g])
        tile = jnp.zeros((8, LANES), jnp.float32)
        for s in range(plane_size):
            found = take(jnp.broadcast_to(plane[g, s : s + 1, :], (8, LANES)), pick)
            keep = ((lane >= s * modes) & (lane < (s + 1) * modes)) | (lane == spread)
            tile = tile + jnp.where(keep, found, 0.0)
        spot = pl.ds(pl.multiple_of(chip * LANES, LANES), LANES)
        column[g, :, spot] = tile
        mine = column.at[g, :, spot]
        for target in column_list:
            send(mine, mine, column_send.at[g], column_recv.at[g], target)
        await_bytes(column.at[g, :, pl.ds(0, (chips - 1) * LANES)], column_recv.at[g])

    def coefficients(g):
        gathered = column[g]
        return [
            [
                jnp.sum(gathered * coarse[s, m : m + 1, :], axis=1, keepdims=True)
                for m in range(modes)
            ]
            for s in range(5)
        ]

    def dot_total(g):
        gathered = column[g]
        total = gathered[:, :LANES]
        for z in range(1, chips):
            total = total + gathered[:, z * LANES : (z + 1) * LANES]
        return jnp.sum(jnp.where(lane == spread, total, 0.0), axis=1, keepdims=True)

    def face(f):
        return slice(f * cap, (f + 1) * cap)

    def correction(coeffs, f):
        total = jnp.zeros((8, cap), jnp.float32)
        for m in range(modes):
            total = total + coeffs[0][m] * own_e[m : m + 1, face(f)]
            total = total + coeffs[1 + f][m] * near_e[m : m + 1, face(f)]
        return total

    def dots(vector):
        return [
            (m, jnp.sum(vector * own_e[m : m + 1, :], axis=1, keepdims=True))
            for m in range(modes)
        ]

    def dot(a, b):
        return (modes, jnp.sum(a * b, axis=1, keepdims=True))

    def partner_tiles(load, start):
        given = [load(c) for c in range(tiles)]
        for b in range(tiles):
            spot = pl.ds(pl.multiple_of(start + b * LANES, LANES), LANES)
            low, high = lo_ref[:, spot], hi_ref[:, spot]
            result = take(given[0], low)
            for c in range(1, tiles):
                result = jnp.where(high == c, take(given[c], low), result)
            yield b, spot, result

    count = count_ref[0, 0]
    rows_pad[...] = jnp.zeros_like(rows_pad)
    rows_pad[0:modes, 0 : loads_ref.shape[1]] = loads_ref[...]
    loads_tile = jnp.where(sub < count, rows_pad[:, :LANES], 0.0)
    first = jnp.zeros((8, LANES), jnp.float32)
    for m in range(modes):
        only = jnp.where(sub == m, loads_tile, 0.0)
        first = first + (only if m == 0 else pltpu.roll(only, 8 * m, axis=1))
    first = jnp.sum(first, axis=0, keepdims=True)

    live_mode = lax.broadcasted_iota(jnp.int32, (modes, cap), 0) < count
    for f in range(4):
        faces_out[f, 0:modes, :] = jnp.where(live_mode, traces_ref[:, face(f)], 0.0)
        faces_out[f, modes : modes + 1, :] = stiff_ref[:, face(f)]
        faces_out[f, modes + 1 : 8, :] = jnp.zeros((7 - modes, cap), jnp.float32)
        faces_out[f, 8:16, :] = rhs_ref[:, face(f)]
    rows_pad[...] = jnp.zeros_like(rows_pad)
    rows_pad[0:modes, :] = inverse_ref[...]
    for z in range(chips):
        start = z * spread
        base, shift = start // LANES, start % LANES
        chunk = rows_pad[:, base * LANES : (base + 1) * LANES]
        if shift:
            chunk = pltpu.roll(chunk, LANES - shift, axis=1)
            if LANES - shift < spread:
                after = rows_pad[:, (base + 1) * LANES : (base + 2) * LANES]
                after = pltpu.roll(after, LANES - shift, axis=1)
                chunk = jnp.where(lane < LANES - shift, chunk, after)
        coarse[0, :, z * LANES : (z + 1) * LANES] = jnp.where(lane < spread, chunk, 0.0)

    pl.semaphore_wait(barrier, len(greeted))

    gather_start(0, first)
    for f in range(4):
        send(faces_out.at[f], faces_in.at[f + 1 - 2 * (f % 2)], setup_send, setup_recv, face_list[f])
    for f in range(4):
        send(coarse.at[0], coarse.at[2 + f - 2 * (f % 2)], coarse_send, coarse_recv, face_list[f])

    for f in range(4):
        index = jnp.broadcast_to(order_ref[f : f + 1, :], (8, cap))
        lo_ref[:, face(f)] = index & (LANES - 1)
        hi_ref[:, face(f)] = index >> 7

    await_bytes(faces_in, setup_recv)

    def setup_face(f, carry):
        start = pl.multiple_of(f * cap, cap)
        length = lengths_ref[0, f]
        for b, spot, other in partner_tiles(
            lambda c: faces_in[f, 0:8, c * LANES : (c + 1) * LANES], start
        ):
            part = slice(b * LANES, (b + 1) * LANES)
            live = lane + b * LANES < length
            mine = faces_out[f, 0:8, part]
            own_e[:, spot] = jnp.where(live, mine, 0.0)
            near_e[:, spot] = jnp.where(live, other, 0.0)
            stiff = jnp.broadcast_to((mine + other)[modes : modes + 1, :], (8, LANES))
            weight[:, spot] = jnp.where(live, 1.0 / jnp.where(live, stiff, 1.0), 0.0)
        for b, spot, other in partner_tiles(
            lambda c: faces_in[f, 8:16, c * LANES : (c + 1) * LANES], start
        ):
            part = slice(b * LANES, (b + 1) * LANES)
            live = lane + b * LANES < length
            known[:, spot] = jnp.where(live, faces_out[f, 8:16, part] + other, 0.0)
        return carry

    lax.fori_loop(0, 4, setup_face, 0)

    half = cap // 2

    def product(vector):
        return lax.dot_general(
            vector.astype(jnp.bfloat16),
            op_v[...],
            (((1,), (1,)), ((), ())),
            preferred_element_type=jnp.float32,
        )

    def exchange(e, rows):
        packed = jnp.concatenate([rows[:, :half], rows[:, half:]], axis=0)
        blocks[e, gz] = packed.astype(jnp.bfloat16)
        mine = blocks.at[e, gz]
        for target in product_list:
            send(mine, blocks.at[e, 4 + opposite(gz)], block_send.at[e], block_recv.at[e], target)
        for target in peer_list:
            send(mine, mine, block_send.at[e], block_recv.at[e], target)
        await_bytes(blocks.at[e, pl.ds(0, 7)], block_recv.at[e])

        def assemble(f, carry):
            start = pl.multiple_of(f * cap, cap)
            length = lengths_ref[0, f]

            def tile_of(slot, c):
                row, at = 8 * (c // (tiles // 2)), (c % (tiles // 2)) * LANES
                return blocks[e, slot, :, at : at + LANES].astype(jnp.float32)[row : row + 8]

            for b, spot, other in partner_tiles(lambda c: tile_of(4 + f, c), start):
                live = lane + b * LANES < length
                image[:, spot] = jnp.where(live, tile_of(f, b) + other, 0.0)
            return carry

        lax.fori_loop(0, 4, assemble, 0)

    gather_finish(0)
    await_bytes(coarse.at[pl.ds(0, 4)], coarse_recv)
    coeffs = coefficients(0)
    for f in range(4):
        out_ref[:, face(f)] = correction(coeffs, f)
    op_copy.wait()
    exchange(0, product(out_ref[...]))
    image[...] = known[...] - image[...]

    gather_start(1, row_of(dots(image[...])))
    gather_finish(1)
    coeffs = coefficients(1)
    for f in range(4):
        resid[:, face(f)] = image[:, face(f)] - correction(coeffs, f)

    scaled = weight[...] * resid[...]
    gather_start(2, row_of(dots(scaled) + [dot(resid[...], scaled)]))
    gather_finish(2)
    coeffs = coefficients(2)
    resid_dot = dot_total(2)
    for f in range(4):
        direct[:, face(f)] = weight[:, face(f)] * resid[:, face(f)] - correction(coeffs, f)
    exchange(1, product(direct[...]))
    gather_start(3, row_of(dots(image[...]) + [dot(direct[...], image[...])]))
    gather_finish(3)
    coeffs = coefficients(3)
    step = resid_dot / dot_total(3)
    for f in range(4):
        out_ref[:, face(f)] = out_ref[:, face(f)] + step * direct[:, face(f)]
        corrected = image[:, face(f)] - correction(coeffs, f)
        resid[:, face(f)] = resid[:, face(f)] - step * corrected

    scaled = weight[...] * resid[...]
    gather_start(4, row_of(dots(scaled) + [dot(resid[...], scaled)]))
    gather_finish(4)
    coeffs = coefficients(4)
    previous, resid_dot = resid_dot, dot_total(4)
    ratio = resid_dot / previous
    for f in range(4):
        projected = weight[:, face(f)] * resid[:, face(f)] - correction(coeffs, f)
        direct[:, face(f)] = projected + ratio * direct[:, face(f)]
    rows = product(direct[...]).astype(jnp.bfloat16).astype(jnp.float32)
    mine = direct[:, pl.ds(pl.multiple_of(gz * cap, cap), cap)]
    peers[pl.ds(gz, 1), :] = row_of([(modes, 2.0 * jnp.sum(mine * rows, axis=1, keepdims=True))])
    spot = peers.at[pl.ds(gz, 1)]
    for target in peer_list:
        send(spot, spot, peer_send, peer_recv, target)
    await_bytes(peers.at[pl.ds(0, nz - 1)], peer_recv)
    gather_start(5, jnp.sum(peers[...], axis=0, keepdims=True))
    gather_finish(5)
    step = resid_dot / dot_total(5)
    for f in range(4):
        out_ref[:, face(f)] = out_ref[:, face(f)] + step * direct[:, face(f)]

    await_bytes(faces_out, setup_send)
    await_bytes(coarse.at[pl.ds(0, 4)], coarse_send)
    await_bytes(peers.at[pl.ds(0, nz - 1)], peer_send)
    for g in range(GATHERS):
        await_bytes(plane.at[g, pl.ds(0, plane_size - 1)], plane_send.at[g])
        await_bytes(column.at[g, :, pl.ds(0, (chips - 1) * LANES)], column_send.at[g])
    for e in range(PRODUCTS):
        await_bytes(blocks.at[e, pl.ds(0, 7)], block_send.at[e])


def solution(mesh):
    sizes = tuple(mesh.shape[axis] for axis in ("gx", "gy", "gz"))
    chips, plane_size = sizes[0] // 2, 2 * sizes[1]

    def shards(
        operator,
        rhs_parts,
        stiffness,
        traces,
        coarse_inverse,
        rigid_loads,
        face_lengths,
        face_order,
        mode_count,
    ):
        rows, order = operator.shape[2:]
        load_count = rhs_parts.shape[2]
        modes = traces.shape[2]
        cap = face_order.shape[3]
        padded = chips * LANES
        f32, i32 = jnp.float32, jnp.int32
        vmem = pl.BlockSpec(memory_space=pltpu.VMEM)
        smem = pl.BlockSpec(memory_space=pltpu.SMEM)
        vector = pltpu.VMEM((load_count, order), f32)
        dma = pltpu.SemaphoreType.DMA
        result = pl.pallas_call(
            functools.partial(kernel, sizes),
            out_shape=jax.ShapeDtypeStruct((load_count, order), f32),
            in_specs=[pl.BlockSpec(memory_space=pl.ANY)] + [vmem] * 5 + [smem, vmem, smem],
            out_specs=vmem,
            scratch_shapes=[
                pltpu.VMEM((rows, order), jnp.bfloat16),
                pltpu.VMEM((4, 16, cap), f32),
                pltpu.VMEM((4, 16, cap), f32),
                pltpu.VMEM((8, coarse_inverse.shape[3]), f32),
                pltpu.VMEM((5, 8, padded), f32),
                pltpu.VMEM((GATHERS, plane_size, LANES), f32),
                pltpu.VMEM((GATHERS, 8, padded), f32),
                pltpu.VMEM((sizes[2], LANES), f32),
                pltpu.VMEM((PRODUCTS, 8, 16, cap // 2), jnp.bfloat16),
                pltpu.VMEM((8, order), i32),
                pltpu.VMEM((8, order), i32),
            ]
            + [vector] * 7
            + [
                dma,
                dma,
                dma,
                dma,
                dma,
                dma((GATHERS,)),
                dma((GATHERS,)),
                dma((GATHERS,)),
                dma((GATHERS,)),
                dma,
                dma,
                dma((PRODUCTS,)),
                dma((PRODUCTS,)),
            ],
            compiler_params=pltpu.CompilerParams(
                collective_id=0, has_side_effects=True, vmem_limit_bytes=40 << 20
            ),
        )(
            operator[0, 0],
            rhs_parts[0, 0],
            stiffness[0],
            traces[0, 0],
            coarse_inverse[0, 0],
            rigid_loads[0, 0],
            face_lengths[0],
            face_order[0, 0],
            mode_count,
        )
        return result[None, None]

    in_specs = (
        P("gx", "gy", "gz", None),
        P("gx", "gy", None, None),
        P("gx", "gy", None),
        P("gx", "gy", None, None),
        P("gx", "gy", None, None),
        P("gx", "gy", None, None),
        P("gx", "gy", None),
        P("gx", "gy", None, None),
        P("gx", "gy"),
    )
    out_specs = P("gx", "gy", None, None)
    return jax.shard_map(shards, mesh=mesh, in_specs=in_specs, out_specs=out_specs, check_vma=False)
```

```python
import functools

import jax
import jax.numpy as jnp
from jax import lax
from jax.experimental import pallas as pl
from jax.experimental.pallas import tpu as pltpu
from jax.sharding import PartitionSpec as P

MESH = pl.DeviceIdType.MESH
GATHERS = 5
PRODUCTS = 2
LANES = 128
STEPS = ((0, 0), (-1, 0), (1, 0), (0, -1), (0, 1))
OFFSETS = STEPS + ((-2, 0), (2, 0), (0, -2), (0, 2), (-1, -1), (-1, 1), (1, -1), (1, 1))


def kernel(
    sizes,
    op_ref,
    rhs_ref,
    stiff_ref,
    traces_ref,
    inverse_ref,
    loads_ref,
    lengths_ref,
    order_ref,
    count_ref,
    out_ref,
    op_v,
    faces_out,
    faces_in,
    rows_pad,
    loads_in,
    loads_pad,
    lengths,
    order_v,
    counts,
    coarse,
    plane,
    column,
    everyone,
    gathered,
    peers,
    pieces,
    tiles_t,
    mixing,
    blocks,
    op_modes,
    lo_ref,
    hi_ref,
    own_e,
    near_e,
    weight,
    known,
    image,
    resid,
    scaled,
    direct,
    second,
    change,
    product_a,
    product_b,
    product_c,
    op_sem,
    in_sem,
    faces_send,
    faces_recv,
    coarse_send,
    coarse_recv,
    plane_send,
    plane_recv,
    column_send,
    column_recv,
    all_send,
    all_recv,
    peer_send,
    peer_recv,
    piece_send,
    piece_recv,
    tile_send,
    tile_recv,
    block_send,
    block_recv,
):
    nx, ny, nz = sizes
    cap = order_ref.shape[1]
    order = rhs_ref.shape[1]
    tiles = cap // LANES
    modes = traces_ref.shape[0]
    chips = nx // 2
    plane_size = 2 * ny
    spread = plane_size * modes
    gx, gy, gz = lax.axis_index("gx"), lax.axis_index("gy"), lax.axis_index("gz")
    chip, core = gx // 2, gx % 2
    f32 = jnp.float32

    def near(face, z):
        sign = 2 * (face % 2) - 1
        along_x = 1 - face // 2
        return (
            lax.rem(gx + along_x * sign + nx, nx),
            lax.rem(gy + (1 - along_x) * sign + ny, ny),
            z,
        )

    def opposite(face):
        return face + 1 - 2 * (face % 2)

    def shifted(dx, dy):
        return (lax.rem(gx + dx + nx, nx), lax.rem(gy + dy + ny, ny), gz)

    def outward(count):
        return [count // 2 + ((j + 1) // 2) * (1 - 2 * (j % 2)) for j in range(count)]

    peer_list = [(gx, gy, lax.rem(gz + k, nz)) for k in (2, 1, 3)]
    plane_list = [
        (chip * 2 + lax.rem(core + 1 - c, 2), lax.rem(gy + k, ny), gz)
        for k in outward(ny)
        for c in range(2)
        if (c == 0) or k
    ]
    column_list = [(lax.rem(gx + 2 * k, nx), gy, gz) for k in outward(chips) if k]
    product_list = [near(gz, k) for k in range(nz)]
    source_list = [near(f, opposite(f)) for f in range(4)]

    op_copy = pltpu.make_async_copy(op_ref, op_v, op_sem)

    def face(f):
        return slice(f * cap, (f + 1) * cap)

    def fetch(src, dst, sem):
        pltpu.make_async_copy(src, dst, sem).start()

    barrier = pltpu.get_barrier_semaphore()
    greeted = (
        [shifted(dx, dy) for dx, dy in OFFSETS[1:]] + peer_list + plane_list + column_list + source_list
    )
    for target in greeted:
        pl.semaphore_signal(barrier, inc=1, device_id=target, device_id_type=MESH)

    fetch(loads_ref, loads_in, in_sem.at[0])
    fetch(count_ref, counts, in_sem.at[1])
    fetch(lengths_ref, lengths, in_sem.at[2])
    fetch(order_ref, order_v, in_sem.at[3])
    for f in range(4):
        spot = pl.ds(f * cap, cap)
        for m in range(modes):
            fetch(traces_ref.at[m, :, spot], faces_out.at[f, pl.ds(m, 1)], in_sem.at[4])
        fetch(stiff_ref.at[:, spot], faces_out.at[f, pl.ds(modes, 1)], in_sem.at[4])
        fetch(rhs_ref.at[:, spot], faces_out.at[f, pl.ds(8, 8)], in_sem.at[5])
    for m in range(modes):
        fetch(inverse_ref.at[m], rows_pad.at[pl.ds(m, 1)], in_sem.at[6])
    op_copy.start()

    sub = lax.broadcasted_iota(jnp.int32, (8, LANES), 0)
    lane = lax.broadcasted_iota(jnp.int32, (8, LANES), 1)

    def send(src, dst, send_sem, recv_sem, target):
        pltpu.make_async_remote_copy(
            src_ref=src,
            dst_ref=dst,
            send_sem=send_sem,
            recv_sem=recv_sem,
            device_id=target,
            device_id_type=MESH,
        ).start()

    def await_bytes(ref, sem):
        pltpu.make_async_copy(ref, ref, sem).wait()

    def share(ref, send_sem, recv_sem):
        mine, facing = ref.at[pl.ds(gz, 1)], ref.at[pl.ds(4 + opposite(gz), 1)]
        for target in product_list:
            send(mine, facing, send_sem, recv_sem, target)
        for target in peer_list:
            send(mine, mine, send_sem, recv_sem, target)

    def take(values, index):
        return jnp.take_along_axis(values, index, axis=1, mode="promise_in_bounds")

    def fold(x):
        total = x[:, :LANES]
        for c in range(1, x.shape[1] // LANES):
            total = total + x[:, c * LANES : (c + 1) * LANES]
        return total

    def across(x):
        return jnp.sum(x, axis=1, keepdims=True)

    def row_of(columns):
        total = jnp.zeros((8, LANES), f32)
        for j, value in enumerate(columns):
            total = total + jnp.where(lane == 8 * j + sub, value, 0.0)
        return jnp.sum(total, axis=0, keepdims=True)

    pick = jnp.minimum(8 * (lane % modes) + sub, LANES - 1)
    my_slot = core * ny + gy
    my_place = gx * ny + gy

    def tile_of_rows(rows):
        tile = take(jnp.broadcast_to(rows(0), (8, LANES)), pick)
        for s in range(1, plane_size):
            found = take(jnp.broadcast_to(rows(s), (8, LANES)), pick)
            tile = jnp.where(lane >= s * modes, found, tile)
        return tile

    def near_gather(row):
        plane[pl.ds(my_slot, 1), :] = row
        mine = plane.at[pl.ds(my_slot, 1)]
        for target in plane_list:
            send(mine, mine, plane_send, plane_recv, target)

    def near_gather_on():
        await_bytes(plane.at[pl.ds(0, plane_size - 1)], plane_recv)
        spot = pl.ds(pl.multiple_of(chip * LANES, LANES), LANES)
        column[:, spot] = tile_of_rows(lambda s: plane[s : s + 1, :])
        mine = column.at[:, spot]
        for target in column_list:
            send(mine, mine, column_send, column_recv, target)

    def near_gather_end():
        await_bytes(column.at[:, pl.ds(0, (chips - 1) * LANES)], column_recv)
        return column[...]

    def gather_start(g, row):
        everyone[g, pl.ds(my_place, 1), :] = row
        mine = everyone.at[g, pl.ds(my_place, 1)]

        def one_plane(i, carry):
            away = chips // 2 + ((i + 1) // 2) * (1 - 2 * (i % 2))
            there = lax.rem(chip + away, chips)
            for k in outward(ny):
                for c in (1, 0):
                    target = (there * 2 + lax.rem(core + c, 2), lax.rem(gy + k, ny), gz)
                    send(mine, mine, all_send.at[g], all_recv.at[g], target)
            return carry

        lax.fori_loop(0, chips - 1, one_plane, 0)
        for target in plane_list:
            send(mine, mine, all_send.at[g], all_recv.at[g], target)

    def gather_wait(g):
        await_bytes(everyone.at[g, pl.ds(0, nx * ny - 1)], all_recv.at[g])

    def gather_end(g):
        gather_wait(g)
        for z in range(chips):
            at = z * plane_size
            gathered[:, z * LANES : (z + 1) * LANES] = tile_of_rows(
                lambda s: everyone[g, at + s : at + s + 1, :]
            )
        return gathered[...]

    def dot_totals(g, wanted):
        total = everyone[g, 0:8, :]
        for c in range(1, nx * ny // 8):
            total = total + everyone[g, 8 * c : 8 * (c + 1), :]
        total = jnp.broadcast_to(jnp.sum(total, axis=0, keepdims=True), (8, LANES))
        return [across(jnp.where(lane == 8 * j + sub, total, 0.0)) for j in wanted]

    def coefficients(values, count):
        return [
            [across(fold(values * coarse[u, m : m + 1, :])) for m in range(modes)]
            for u in range(count)
        ]

    def correction(coeffs, f):
        total = coeffs[0][0] * own_e[0:1, face(f)]
        total = total + coeffs[1 + f][0] * near_e[0:1, face(f)]
        for m in range(1, modes):
            total = total + coeffs[0][m] * own_e[m : m + 1, face(f)]
            total = total + coeffs[1 + f][m] * near_e[m : m + 1, face(f)]
        return total

    def corrected_product(coeffs):
        total = coeffs[0][0] * op_modes[0:1, :]
        for u in range(5):
            for m in range(modes):
                if u or m:
                    total = total + coeffs[u][m] * op_modes[8 * u + m : 8 * u + m + 1, :]
        return total

    where_of = {offset: u for u, offset in enumerate(OFFSETS)}
    own_lane = (lane % 8 == sub) & (lane < 8 * modes)

    def mixed_row(coeffs):
        total = jnp.zeros((8, LANES), f32)
        for t, at in enumerate(STEPS):
            for u, step in enumerate(STEPS):
                found = coeffs[where_of[(at[0] + step[0], at[1] + step[1])]]
                for m in range(modes):
                    total = total + found[m] * mixing[t, 8 * u + m : 8 * u + m + 1, :]
        return jnp.sum(jnp.where(own_lane, total, 0.0), axis=0, keepdims=True)

    def partner_tiles(load, start):
        given = [load(c) for c in range(tiles)]
        for b in range(tiles):
            spot = pl.ds(pl.multiple_of(start + b * LANES, LANES), LANES)
            low, high = lo_ref[:, spot], hi_ref[:, spot]
            result = take(given[0], low)
            for c in range(1, tiles):
                result = jnp.where(high == c, take(given[c], low), result)
            yield b, spot, result

    def split(x):
        high = x.astype(jnp.bfloat16)
        low = (x - high.astype(f32)).astype(jnp.bfloat16)
        return jnp.concatenate([high.astype(f32), low.astype(f32)], axis=0).astype(jnp.bfloat16)

    def times(left, columns):
        return lax.dot_general(
            left, op_v[:, columns], (((1,), (1,)), ((), ())), preferred_element_type=f32
        )

    def product(vector):
        total = jnp.zeros((8, cap), f32)
        for f in range(4):
            both = times(split(vector[:, face(f)]), face(f))
            total = total + both[:8] + both[8:]
        return total

    def exchange_start(e, rows):
        blocks[e, pl.ds(gz, 1)] = rows.reshape(1, 8, cap)
        share(blocks.at[e], block_send.at[e], block_recv.at[e])

    def exchange_end(e, use):
        await_bytes(blocks.at[e, pl.ds(0, 7)], block_recv.at[e])

        def assemble(f, carry):
            start = pl.multiple_of(f * cap, cap)
            length = lengths[0, f]

            def tile_of(slot, c):
                return blocks[e, slot, :, c * LANES : (c + 1) * LANES]

            for b, spot, other in partner_tiles(lambda c: tile_of(4 + f, c), start):
                live = lane + b * LANES < length
                use(spot, jnp.where(live, tile_of(f, b) + other, 0.0))
            return carry

        lax.fori_loop(0, 4, assemble, 0)

    await_bytes(loads_in, in_sem.at[0])
    await_bytes(counts, in_sem.at[1])
    count = counts[0, 0]
    loads_pad[...] = jnp.zeros_like(loads_pad)
    for m in range(modes):
        loads_pad[m : m + 1, 0 : loads_ref.shape[2]] = loads_in[m]
    loads_tile = jnp.where(sub < count, loads_pad[...], 0.0)
    first = jnp.zeros((8, LANES), f32)
    for m in range(modes):
        only = jnp.where(sub == m, loads_tile, 0.0)
        first = first + (only if m == 0 else pltpu.roll(only, 8 * m, axis=1))
    first = jnp.sum(first, axis=0, keepdims=True)

    await_bytes(faces_out.at[:, pl.ds(0, modes + 1)], in_sem.at[4])
    await_bytes(faces_out.at[:, pl.ds(8, 8)], in_sem.at[5])
    live_mode = lax.broadcasted_iota(jnp.int32, (modes, cap), 0) < count
    for f in range(4):
        faces_out[f, 0:modes, :] = jnp.where(live_mode, faces_out[f, 0:modes, :], 0.0)
        faces_out[f, modes + 1 : 8, :] = jnp.zeros((7 - modes, cap), f32)

    pl.semaphore_wait(barrier, len(greeted))

    near_gather(first)
    for f in range(4):
        send(
            faces_out.at[f], faces_in.at[f + 1 - 2 * (f % 2)], faces_send, faces_recv, near(f, gz)
        )

    await_bytes(rows_pad.at[pl.ds(0, modes)], in_sem.at[6])
    rows_pad[modes:8, :] = jnp.zeros((8 - modes, rows_pad.shape[1]), f32)
    for z in range(chips):
        start = z * spread
        base, shift = start // LANES, start % LANES
        chunk = rows_pad[:, base * LANES : (base + 1) * LANES]
        if shift:
            chunk = pltpu.roll(chunk, LANES - shift, axis=1)
            if LANES - shift < spread:
                after = rows_pad[:, (base + 1) * LANES : (base + 2) * LANES]
                after = pltpu.roll(after, LANES - shift, axis=1)
                chunk = jnp.where(lane < LANES - shift, chunk, after)
        coarse[0, :, z * LANES : (z + 1) * LANES] = jnp.where(lane < spread, chunk, 0.0)
    for u in range(1, len(OFFSETS)):
        dx, dy = OFFSETS[u]
        send(
            coarse.at[0, pl.ds(0, modes)],
            coarse.at[u, pl.ds(0, modes)],
            coarse_send,
            coarse_recv,
            shifted(-dx, -dy),
        )

    await_bytes(lengths, in_sem.at[2])
    await_bytes(order_v, in_sem.at[3])
    for f in range(4):
        index = jnp.broadcast_to(order_v[f : f + 1, :], (8, cap))
        lo_ref[:, face(f)] = index & (LANES - 1)
        hi_ref[:, face(f)] = index >> 7

    await_bytes(faces_in, faces_recv)

    def setup_face(f, carry):
        start = pl.multiple_of(f * cap, cap)
        length = lengths[0, f]
        for b, spot, other in partner_tiles(
            lambda c: faces_in[f, 0:8, c * LANES : (c + 1) * LANES], start
        ):
            part = slice(b * LANES, (b + 1) * LANES)
            live = lane + b * LANES < length
            mine = faces_out[f, 0:8, part]
            own_e[:, spot] = jnp.where(live & (sub < modes), mine, 0.0)
            near_e[:, spot] = jnp.where(live & (sub < modes), other, 0.0)
            stiff = jnp.broadcast_to((mine + other)[modes : modes + 1, :], (8, LANES))
            weight[:, spot] = jnp.where(live, 1.0 / jnp.where(live, stiff, 1.0), 0.0)
        for b, spot, other in partner_tiles(
            lambda c: faces_in[f, 8:16, c * LANES : (c + 1) * LANES], start
        ):
            part = slice(b * LANES, (b + 1) * LANES)
            live = lane + b * LANES < length
            known[:, spot] = jnp.where(live, faces_out[f, 8:16, part] + other, 0.0)
        return carry

    lax.fori_loop(0, 4, setup_face, 0)
    near_gather_on()

    op_copy.wait()
    own_rows = jnp.zeros((8, cap), f32)
    for f in range(4):
        both = jnp.concatenate([own_e[:, face(f)], near_e[:, face(f)]], axis=0)
        both = times(split(both), face(f))
        both = both[:16] + both[16:]
        own_rows = own_rows + both[:8]
        op_modes[8 * (1 + f) : 8 * (2 + f), :] = both[8:]
    op_modes[0:8, :] = own_rows

    block = pl.ds(pl.multiple_of(gz * cap, cap), cap)
    block_e = jnp.concatenate([own_e[:, block], near_e[:, block]], axis=0)
    part = lax.dot_general(
        op_modes[...],
        block_e,
        (((1,), (1,)), ((), ())),
        precision=lax.Precision.HIGHEST,
        preferred_element_type=f32,
    )
    wide = jnp.concatenate([part, jnp.zeros((40, LANES - 16), f32)], axis=1)
    tiles_t[pl.ds(gz, 1)] = wide.reshape(1, 40, LANES)
    share(tiles_t, tile_send, tile_recv)
    known_dots = [
        across(sum(fold(known[:, face(f)] * own_e[m : m + 1, face(f)]) for f in range(4)))
        for m in range(modes)
    ]
    known_row = row_of(known_dots)
    await_bytes(tiles_t.at[pl.ds(0, 7)], tile_recv)
    spread_own = jnp.minimum(lane // 8, 7)
    for u in range(5):
        rows = slice(8 * u, 8 * (u + 1))
        own_sum = tiles_t[0, rows, :] + tiles_t[1, rows, :] + tiles_t[2, rows, :] + tiles_t[3, rows, :]
        mixing[0, rows, :] = take(own_sum, spread_own)
        for f in range(4):
            mixing[1 + f, rows, :] = take(tiles_t[4 + f, rows, :], spread_own + 8)

    await_bytes(coarse.at[pl.ds(0, len(OFFSETS) - 1), pl.ds(0, modes)], coarse_recv)
    coeffs = coefficients(near_gather_end(), len(OFFSETS))
    gather_start(0, known_row - mixed_row(coeffs))
    exchange_start(0, corrected_product(coeffs))
    for f in range(4):
        out_ref[:, face(f)] = correction(coeffs, f)

    def gap(spot, tile):
        image[:, spot] = known[:, spot] - tile

    exchange_end(0, gap)

    coeffs = coefficients(gather_end(0), 5)
    sums = [jnp.zeros((8, LANES), f32) for _ in range(modes + 1)]
    for f in range(4):
        left = image[:, face(f)] - correction(coeffs, f)
        right = weight[:, face(f)] * left
        resid[:, face(f)] = left
        scaled[:, face(f)] = right
        for m in range(modes):
            sums[m] = sums[m] + fold(right * own_e[m : m + 1, face(f)])
        sums[modes] = sums[modes] + fold(left * right)
    gather_start(1, row_of([across(x) for x in sums]))

    rows = product(scaled)
    product_a[...] = rows
    parts = [
        across(fold(rows * e[m : m + 1, block])) for e in (own_e, near_e) for m in range(modes)
    ]
    pieces[pl.ds(gz, 1), :] = row_of(parts)
    share(pieces, piece_send, piece_recv)
    await_bytes(pieces.at[pl.ds(0, 7)], piece_recv)
    found = pieces[...]
    found = jnp.where(sub < 4, found, pltpu.roll(found, LANES - 8 * modes, axis=1))
    found = jnp.where(lane < 8 * modes, found, 0.0)
    found = jnp.sum(found, axis=0, keepdims=True)

    first_coeffs = coefficients(gather_end(1), len(OFFSETS))
    gather_start(2, found - mixed_row(first_coeffs))
    (resid_dot,) = dot_totals(1, (modes,))
    rows = product_a[...] - corrected_product(first_coeffs)
    product_b[...] = rows
    exchange_start(1, rows)
    for f in range(4):
        direct[:, face(f)] = scaled[:, face(f)] - correction(first_coeffs, f)

    def keep(spot, tile):
        image[:, spot] = tile

    exchange_end(1, keep)

    coeffs = coefficients(gather_end(2), 5)
    sums = [jnp.zeros((8, LANES), f32) for _ in range(modes + 3)]
    for f in range(4):
        left = image[:, face(f)] - correction(coeffs, f)
        right = weight[:, face(f)] * left
        change[:, face(f)] = right
        for m in range(modes):
            sums[m] = sums[m] + fold(right * own_e[m : m + 1, face(f)])
        sums[modes] = sums[modes] + fold(direct[:, face(f)] * image[:, face(f)])
        sums[modes + 1] = sums[modes + 1] + fold(resid[:, face(f)] * right)
        sums[modes + 2] = sums[modes + 2] + fold(left * right)
    gather_start(3, row_of([across(x) for x in sums]))
    product_c[...] = product(change)

    change_coeffs = coefficients(gather_end(3), 5)
    curvature, cross, square = dot_totals(3, (modes, modes + 1, modes + 2))
    step = resid_dot / curvature
    next_dot = resid_dot - 2.0 * step * cross + step * step * square
    ratio = next_dot / resid_dot
    coeffs = [
        [a - step * b for a, b in zip(first_coeffs[u], change_coeffs[u], strict=True)]
        for u in range(5)
    ]
    for f in range(4):
        projected = scaled[:, face(f)] - step * change[:, face(f)] - correction(coeffs, f)
        second[:, face(f)] = projected + ratio * direct[:, face(f)]
    rows = product_a[...] - step * product_c[...] - corrected_product(coeffs)
    rows = rows + ratio * product_b[...]
    half = across(fold(second[:, block] * rows))
    peers[pl.ds(gz, 1), :] = row_of([jnp.zeros((8, 1), f32)] * modes + [2.0 * half])
    mine = peers.at[pl.ds(gz, 1)]
    for target in peer_list:
        send(mine, mine, peer_send, peer_recv, target)
    await_bytes(peers.at[pl.ds(0, nz - 1)], peer_recv)
    gather_start(4, jnp.sum(peers[...], axis=0, keepdims=True))
    for f in range(4):
        out_ref[:, face(f)] = out_ref[:, face(f)] + step * direct[:, face(f)]
    gather_wait(4)
    (curvature,) = dot_totals(4, (modes,))
    step = next_dot / curvature
    for f in range(4):
        out_ref[:, face(f)] = out_ref[:, face(f)] + step * second[:, face(f)]

    await_bytes(faces_out, faces_send)
    await_bytes(coarse.at[pl.ds(0, len(OFFSETS) - 1), pl.ds(0, modes)], coarse_send)
    await_bytes(plane.at[pl.ds(0, plane_size - 1)], plane_send)
    await_bytes(column.at[:, pl.ds(0, (chips - 1) * LANES)], column_send)
    await_bytes(peers.at[pl.ds(0, nz - 1)], peer_send)
    await_bytes(pieces.at[pl.ds(0, 7)], piece_send)
    await_bytes(tiles_t.at[pl.ds(0, 7)], tile_send)
    for g in range(GATHERS):
        await_bytes(everyone.at[g, pl.ds(0, nx * ny - 1)], all_send.at[g])
    for e in range(PRODUCTS):
        await_bytes(blocks.at[e, pl.ds(0, 7)], block_send.at[e])


def solution(mesh):
    sizes = tuple(mesh.shape[axis] for axis in ("gx", "gy", "gz"))
    chips, plane_size = sizes[0] // 2, 2 * sizes[1]

    def shards(
        operator,
        rhs_parts,
        stiffness,
        traces,
        coarse_inverse,
        rigid_loads,
        face_lengths,
        face_order,
        mode_count,
    ):
        rows, order = operator.shape[2:]
        load_count = rhs_parts.shape[2]
        modes = traces.shape[2]
        cap = face_order.shape[3]
        padded = chips * LANES
        f32, i32 = jnp.float32, jnp.int32
        anywhere = pl.BlockSpec(memory_space=pl.ANY)
        vector = pltpu.VMEM((load_count, order), f32)
        block = pltpu.VMEM((load_count, cap), f32)
        dma = pltpu.SemaphoreType.DMA

        def by_row(array):
            return jnp.transpose(array[0], (1, 0, 2))

        result = pl.pallas_call(
            functools.partial(kernel, sizes),
            out_shape=jax.ShapeDtypeStruct((load_count, order), f32),
            in_specs=[anywhere] * 9,
            out_specs=pl.BlockSpec(memory_space=pltpu.VMEM),
            scratch_shapes=[
                pltpu.VMEM((rows, order), jnp.bfloat16),
                pltpu.VMEM((4, 16, cap), f32),
                pltpu.VMEM((4, 16, cap), f32),
                pltpu.VMEM((8, coarse_inverse.shape[3]), f32),
                pltpu.VMEM((modes, 1, load_count), f32),
                pltpu.VMEM((8, LANES), f32),
                pltpu.SMEM((1, 4), i32),
                pltpu.VMEM((4, cap), i32),
                pltpu.SMEM((1, 1), i32),
                pltpu.VMEM((len(OFFSETS), 8, padded), f32),
                pltpu.VMEM((plane_size, LANES), f32),
                pltpu.VMEM((8, padded), f32),
                pltpu.VMEM((GATHERS, sizes[0] * sizes[1], LANES), f32),
                pltpu.VMEM((8, padded), f32),
                pltpu.VMEM((sizes[2], LANES), f32),
                pltpu.VMEM((8, LANES), f32),
                pltpu.VMEM((8, 40, LANES), f32),
                pltpu.VMEM((5, 40, LANES), f32),
                pltpu.VMEM((PRODUCTS, 8, 8, cap), f32),
                pltpu.VMEM((40, cap), f32),
                pltpu.VMEM((8, order), i32),
                pltpu.VMEM((8, order), i32),
            ]
            + [vector] * 10
            + [block] * 3
            + [dma, dma((7,))]
            + [dma] * 8
            + [dma((GATHERS,))] * 2
            + [dma] * 6
            + [dma((PRODUCTS,))] * 2,
            compiler_params=pltpu.CompilerParams(
                collective_id=0, has_side_effects=True, vmem_limit_bytes=60 << 20
            ),
        )(
            operator[0, 0],
            rhs_parts[0, 0],
            stiffness[0],
            by_row(traces),
            by_row(coarse_inverse),
            by_row(rigid_loads),
            face_lengths[0],
            face_order[0, 0],
            mode_count,
        )
        return result[None, None]

    in_specs = (
        P("gx", "gy", "gz", None),
        P("gx", "gy", None, None),
        P("gx", "gy", None),
        P("gx", "gy", None, None),
        P("gx", "gy", None, None),
        P("gx", "gy", None, None),
        P("gx", "gy", None),
        P("gx", "gy", None, None),
        P("gx", "gy"),
    )
    out_specs = P("gx", "gy", None, None)
    return jax.shard_map(shards, mesh=mesh, in_specs=in_specs, out_specs=out_specs, check_vma=False)
```

```python
import functools

import jax
import jax.numpy as jnp
from jax import lax
from jax.experimental import pallas as pl
from jax.experimental.pallas import tpu as pltpu
from jax.sharding import PartitionSpec as P

MESH = pl.DeviceIdType.MESH
GATHERS = 4
PRODUCTS = 2
LANES = 128
STEPS = ((0, 0), (-1, 0), (1, 0), (0, -1), (0, 1))
OFFSETS = STEPS + ((-2, 0), (2, 0), (0, -2), (0, 2), (-1, -1), (-1, 1), (1, -1), (1, 1))


def kernel(
    sizes,
    op_ref,
    rhs_ref,
    stiff_ref,
    traces_ref,
    inverse_ref,
    loads_ref,
    lengths_ref,
    order_ref,
    count_ref,
    out_ref,
    op_v,
    faces_out,
    faces_in,
    rows_pad,
    loads_in,
    loads_pad,
    lengths,
    order_v,
    counts,
    coarse,
    plane,
    column,
    everyone,
    peers,
    tiles_t,
    mixing,
    blocks,
    op_modes,
    op_heavy,
    chunks,
    plane_sc,
    parts_out,
    parts_in,
    twice,
    lo_ref,
    hi_ref,
    own_e,
    near_e,
    weight,
    known,
    image,
    resid,
    scaled,
    direct,
    second,
    change,
    product_a,
    product_b,
    product_c,
    op_sem,
    in_sem,
    faces_send,
    faces_recv,
    coarse_send,
    coarse_recv,
    plane_send,
    plane_recv,
    column_send,
    column_recv,
    all_send,
    all_recv,
    peer_send,
    peer_recv,
    tile_send,
    tile_recv,
    block_send,
    block_recv,
    chunk_send,
    chunk_recv,
    sc_send,
    sc_recv,
    parts_send,
    parts_recv,
    twice_send,
    twice_recv,
):
    nx, ny, nz = sizes
    cap = order_ref.shape[1]
    order = rhs_ref.shape[1]
    tiles = cap // LANES
    modes = traces_ref.shape[0]
    chips = nx // 2
    plane_size = 2 * ny
    spread = plane_size * modes
    gx, gy, gz = lax.axis_index("gx"), lax.axis_index("gy"), lax.axis_index("gz")
    chip, core = gx // 2, gx % 2
    f32 = jnp.float32

    def near(face, z):
        sign = 2 * (face % 2) - 1
        along_x = 1 - face // 2
        return (
            lax.rem(gx + along_x * sign + nx, nx),
            lax.rem(gy + (1 - along_x) * sign + ny, ny),
            z,
        )

    def opposite(face):
        return face + 1 - 2 * (face % 2)

    def shifted(dx, dy):
        return (lax.rem(gx + dx + nx, nx), lax.rem(gy + dy + ny, ny), gz)

    def outward(count):
        return [count // 2 + ((j + 1) // 2) * (1 - 2 * (j % 2)) for j in range(count)]

    peer_list = [(gx, gy, lax.rem(gz + k, nz)) for k in (2, 1, 3)]
    plane_list = [
        (chip * 2 + lax.rem(core + 1 - c, 2), lax.rem(gy + k, ny), gz)
        for k in outward(ny)
        for c in range(2)
        if (c == 0) or k
    ]
    column_list = [(lax.rem(gx + 2 * k, nx), gy, gz) for k in outward(chips) if k]
    product_list = [near(gz, k) for k in range(nz)]
    source_list = [near(f, opposite(f)) for f in range(4)]

    op_copy = pltpu.make_async_copy(op_ref, op_v, op_sem)

    def face(f):
        return slice(f * cap, (f + 1) * cap)

    def fetch(src, dst, sem):
        pltpu.make_async_copy(src, dst, sem).start()

    barrier = pltpu.get_barrier_semaphore()
    greeted = (
        [shifted(dx, dy) for dx, dy in OFFSETS[1:]] + peer_list + plane_list + column_list + source_list
    )
    for target in greeted:
        pl.semaphore_signal(barrier, inc=1, device_id=target, device_id_type=MESH)

    fetch(loads_ref, loads_in, in_sem.at[0])
    fetch(count_ref, counts, in_sem.at[1])
    fetch(lengths_ref, lengths, in_sem.at[2])
    fetch(order_ref, order_v, in_sem.at[3])
    for f in range(4):
        spot = pl.ds(f * cap, cap)
        for m in range(modes):
            fetch(traces_ref.at[m, :, spot], faces_out.at[f, pl.ds(m, 1)], in_sem.at[4])
        fetch(stiff_ref.at[:, spot], faces_out.at[f, pl.ds(modes, 1)], in_sem.at[4])
        fetch(rhs_ref.at[:, spot], faces_out.at[f, pl.ds(8, 8)], in_sem.at[5])
    for m in range(modes):
        fetch(inverse_ref.at[m], rows_pad.at[pl.ds(m, 1)], in_sem.at[6])
    op_copy.start()

    sub = lax.broadcasted_iota(jnp.int32, (8, LANES), 0)
    lane = lax.broadcasted_iota(jnp.int32, (8, LANES), 1)

    def send(src, dst, send_sem, recv_sem, target):
        pltpu.make_async_remote_copy(
            src_ref=src,
            dst_ref=dst,
            send_sem=send_sem,
            recv_sem=recv_sem,
            device_id=target,
            device_id_type=MESH,
        ).start()

    def await_bytes(ref, sem):
        pltpu.make_async_copy(ref, ref, sem).wait()

    def share(ref, send_sem, recv_sem):
        mine, facing = ref.at[pl.ds(gz, 1)], ref.at[pl.ds(4 + opposite(gz), 1)]
        for target in product_list:
            send(mine, facing, send_sem, recv_sem, target)
        for target in peer_list:
            send(mine, mine, send_sem, recv_sem, target)

    def take(values, index):
        return jnp.take_along_axis(values, index, axis=1, mode="promise_in_bounds")

    def fold(x):
        total = x[:, :LANES]
        for c in range(1, x.shape[1] // LANES):
            total = total + x[:, c * LANES : (c + 1) * LANES]
        return total

    def across(x):
        return jnp.sum(x, axis=1, keepdims=True)

    def row_of(columns):
        total = jnp.zeros((8, LANES), f32)
        for j, value in enumerate(columns):
            if value is None:
                continue
            total = total + jnp.where(lane == 8 * j + sub, value, 0.0)
        return jnp.sum(total, axis=0, keepdims=True)

    pick = jnp.minimum(8 * (lane % modes) + sub, LANES - 1)
    my_slot = core * ny + gy

    def tile_of_rows(rows, first=0):
        at = jnp.minimum(pick + 8 * first, LANES - 1)
        tile = take(jnp.broadcast_to(rows(0), (8, LANES)), at)
        for s in range(1, plane_size):
            found = take(jnp.broadcast_to(rows(s), (8, LANES)), at)
            tile = jnp.where(lane >= s * modes, found, tile)
        return tile

    def near_gather(row):
        plane[pl.ds(my_slot, 1), :] = row
        mine = plane.at[pl.ds(my_slot, 1)]
        for target in plane_list:
            send(mine, mine, plane_send, plane_recv, target)

    def near_gather_on():
        await_bytes(plane.at[pl.ds(0, plane_size - 1)], plane_recv)
        spot = pl.ds(pl.multiple_of(chip * LANES, LANES), LANES)
        column[:, spot] = tile_of_rows(lambda s: plane[s : s + 1, :])
        mine = column.at[:, spot]
        for target in column_list:
            send(mine, mine, column_send, column_recv, target)

    def near_gather_end():
        await_bytes(column.at[:, pl.ds(0, (chips - 1) * LANES)], column_recv)
        return column[...]

    pair = 2 * (chip * ny + gy)

    def gather_start(g, row):
        everyone[g, pl.ds(pair + core, 1), :] = row
        mine = everyone.at[g, pl.ds(pair + core, 1)]

        def one_plane(i, carry):
            away = chips // 2 + ((i + 1) // 2) * (1 - 2 * (i % 2))
            there = lax.rem(chip + away, chips)
            for k in outward(ny):
                for c in (1, 0):
                    target = (there * 2 + lax.rem(core + c, 2), lax.rem(gy + k, ny), gz)
                    send(mine, mine, all_send.at[g], all_recv.at[g], target)
            return carry

        lax.fori_loop(0, chips - 1, one_plane, 0)
        for target in plane_list:
            send(mine, mine, all_send.at[g], all_recv.at[g], target)

    def gather_wait(g):
        await_bytes(everyone.at[g, pl.ds(0, nx * ny - 1)], all_recv.at[g])

    def coarse_values(g, first=0):
        planes = []
        for z in range(chips):
            at = z * plane_size
            planes.append(
                tile_of_rows(
                    lambda s: everyone[g, pl.ds(at + 2 * (s % ny) + s // ny, 1), :], first
                )
            )
        return jnp.concatenate(planes, axis=1)

    def dot_totals(g, wanted):
        total = everyone[g, 0:8, :]
        for c in range(1, nx * ny // 8):
            total = total + everyone[g, 8 * c : 8 * (c + 1), :]
        total = jnp.broadcast_to(jnp.sum(total, axis=0, keepdims=True), (8, LANES))
        return [across(jnp.where(lane == 8 * j + sub, total, 0.0)) for j in wanted]

    def coefficients(values, count):
        return [
            [across(fold(values * coarse[u, m : m + 1, :])) for m in range(modes)]
            for u in range(count)
        ]

    def correction(coeffs, f):
        total = coeffs[0][0] * own_e[0:1, face(f)]
        total = total + coeffs[1 + f][0] * near_e[0:1, face(f)]
        for m in range(1, modes):
            total = total + coeffs[0][m] * own_e[m : m + 1, face(f)]
            total = total + coeffs[1 + f][m] * near_e[m : m + 1, face(f)]
        return total

    def modes_times(ref, coeffs):
        total = coeffs[0][0] * ref[0:1, :]
        for u in range(5):
            for m in range(modes):
                if u or m:
                    total = total + coeffs[u][m] * ref[8 * u + m : 8 * u + m + 1, :]
        return total

    where_of = {offset: u for u, offset in enumerate(OFFSETS)}
    own_lane = (lane % 8 == sub) & (lane < 8 * modes)

    def mixed_row(coeffs):
        total = jnp.zeros((8, LANES), f32)
        for t, at in enumerate(STEPS):
            for u, step in enumerate(STEPS):
                found = coeffs[where_of[(at[0] + step[0], at[1] + step[1])]]
                for m in range(modes):
                    total = total + found[m] * mixing[t, 8 * u + m : 8 * u + m + 1, :]
        return jnp.sum(jnp.where(own_lane, total, 0.0), axis=0, keepdims=True)

    def partner_tiles(load, start):
        given = [load(c) for c in range(tiles)]
        for b in range(tiles):
            spot = pl.ds(pl.multiple_of(start + b * LANES, LANES), LANES)
            low, high = lo_ref[:, spot], hi_ref[:, spot]
            result = take(given[0], low)
            for c in range(1, tiles):
                result = jnp.where(high == c, take(given[c], low), result)
            yield b, spot, result

    def split(x):
        high = x.astype(jnp.bfloat16)
        low = (x - high.astype(f32)).astype(jnp.bfloat16)
        return jnp.concatenate([high.astype(f32), low.astype(f32)], axis=0).astype(jnp.bfloat16)

    def times(left, columns):
        return lax.dot_general(
            left, op_v[:, columns], (((1,), (1,)), ((), ())), preferred_element_type=f32
        )

    def product(vector):
        total = jnp.zeros((8, cap), f32)
        for f in range(4):
            both = times(split(vector[:, face(f)]), face(f))
            total = total + both[:8] + both[8:]
        return total

    def exchange_start(e, rows):
        packed = jnp.concatenate([rows[:, : cap // 2], rows[:, cap // 2 :]], axis=0)
        blocks[e, pl.ds(gz, 1)] = packed.astype(jnp.bfloat16).reshape(1, 16, cap // 2)
        share(blocks.at[e], block_send.at[e], block_recv.at[e])

    def exchange_end(e, use):
        await_bytes(blocks.at[e, pl.ds(0, 7)], block_recv.at[e])

        def assemble(f, carry):
            start = pl.multiple_of(f * cap, cap)
            length = lengths[0, f]

            def tile_of(slot, c):
                row, at = 8 * (c // (tiles // 2)), c % (tiles // 2) * LANES
                both = blocks[e, slot, :, at : at + LANES].astype(f32)
                return both[row : row + 8]

            for b, spot, other in partner_tiles(lambda c: tile_of(4 + f, c), start):
                live = lane + b * LANES < length
                use(spot, jnp.where(live, tile_of(f, b) + other, 0.0))
            return carry

        lax.fori_loop(0, 4, assemble, 0)

    await_bytes(loads_in, in_sem.at[0])
    await_bytes(counts, in_sem.at[1])
    count = counts[0, 0]
    loads_pad[...] = jnp.zeros_like(loads_pad)
    for m in range(modes):
        loads_pad[m : m + 1, 0 : loads_ref.shape[2]] = loads_in[m]
    loads_tile = jnp.where(sub < count, loads_pad[...], 0.0)
    first = jnp.zeros((8, LANES), f32)
    for m in range(modes):
        only = jnp.where(sub == m, loads_tile, 0.0)
        first = first + (only if m == 0 else pltpu.roll(only, 8 * m, axis=1))
    first = jnp.sum(first, axis=0, keepdims=True)

    await_bytes(faces_out.at[:, pl.ds(0, modes + 1)], in_sem.at[4])
    await_bytes(faces_out.at[:, pl.ds(8, 8)], in_sem.at[5])
    live_mode = lax.broadcasted_iota(jnp.int32, (modes, cap), 0) < count
    for f in range(4):
        faces_out[f, 0:modes, :] = jnp.where(live_mode, faces_out[f, 0:modes, :], 0.0)
        faces_out[f, modes + 1 : 8, :] = jnp.zeros((7 - modes, cap), f32)

    pl.semaphore_wait(barrier, len(greeted))

    near_gather(first)
    for f in range(4):
        send(
            faces_out.at[f], faces_in.at[f + 1 - 2 * (f % 2)], faces_send, faces_recv, near(f, gz)
        )

    await_bytes(rows_pad.at[pl.ds(0, modes)], in_sem.at[6])
    rows_pad[modes:8, :] = jnp.zeros((8 - modes, rows_pad.shape[1]), f32)
    for z in range(chips):
        start = z * spread
        base, shift = start // LANES, start % LANES
        chunk = rows_pad[:, base * LANES : (base + 1) * LANES]
        if shift:
            chunk = pltpu.roll(chunk, LANES - shift, axis=1)
            if LANES - shift < spread:
                after = rows_pad[:, (base + 1) * LANES : (base + 2) * LANES]
                after = pltpu.roll(after, LANES - shift, axis=1)
                chunk = jnp.where(lane < LANES - shift, chunk, after)
        coarse[0, :, z * LANES : (z + 1) * LANES] = jnp.where(lane < spread, chunk, 0.0)
    for u in range(1, len(OFFSETS)):
        dx, dy = OFFSETS[u]
        send(
            coarse.at[0, pl.ds(0, modes)],
            coarse.at[u, pl.ds(0, modes)],
            coarse_send,
            coarse_recv,
            shifted(-dx, -dy),
        )

    chunks[pl.ds(chip, 1)] = coarse[
        0, :, pl.ds(pl.multiple_of(chip * LANES, LANES), LANES)
    ].reshape(1, 8, LANES)
    for k in outward(chips):
        if k:
            there = lax.rem(chip + k, chips)
            send(
                coarse.at[0, :, pl.ds(pl.multiple_of(there * LANES, LANES), LANES)],
                chunks.at[chip],
                chunk_send,
                chunk_recv,
                (there * 2 + core, gy, gz),
            )
    await_bytes(lengths, in_sem.at[2])
    await_bytes(order_v, in_sem.at[3])
    for f in range(4):
        index = jnp.broadcast_to(order_v[f : f + 1, :], (8, cap))
        lo_ref[:, face(f)] = index & (LANES - 1)
        hi_ref[:, face(f)] = index >> 7

    await_bytes(faces_in, faces_recv)

    def setup_face(f, carry):
        start = pl.multiple_of(f * cap, cap)
        length = lengths[0, f]
        for b, spot, other in partner_tiles(
            lambda c: faces_in[f, 0:8, c * LANES : (c + 1) * LANES], start
        ):
            part = slice(b * LANES, (b + 1) * LANES)
            live = lane + b * LANES < length
            mine = faces_out[f, 0:8, part]
            own_e[:, spot] = jnp.where(live & (sub < modes), mine, 0.0)
            near_e[:, spot] = jnp.where(live & (sub < modes), other, 0.0)
            stiff = jnp.broadcast_to((mine + other)[modes : modes + 1, :], (8, LANES))
            weight[:, spot] = jnp.where(live, 1.0 / jnp.where(live, stiff, 1.0), 0.0)
        for b, spot, other in partner_tiles(
            lambda c: faces_in[f, 8:16, c * LANES : (c + 1) * LANES], start
        ):
            part = slice(b * LANES, (b + 1) * LANES)
            live = lane + b * LANES < length
            known[:, spot] = jnp.where(live, faces_out[f, 8:16, part] + other, 0.0)
        return carry

    lax.fori_loop(0, 4, setup_face, 0)
    near_gather_on()

    def modes_product(ref, heavy):
        own_rows = jnp.zeros((8, cap), f32)
        for f in range(4):
            both = [own_e[:, face(f)], near_e[:, face(f)]]
            if heavy:
                both = [weight[:, face(f)] * e for e in both]
            both = times(split(jnp.concatenate(both, axis=0)), face(f))
            both = both[:16] + both[16:]
            own_rows = own_rows + both[:8]
            ref[8 * (1 + f) : 8 * (2 + f), :] = both[8:]
        ref[0:8, :] = own_rows

    op_copy.wait()
    modes_product(op_modes, False)

    block = pl.ds(pl.multiple_of(gz * cap, cap), cap)
    block_e = jnp.concatenate([own_e[:, block], near_e[:, block]], axis=0)
    part = lax.dot_general(
        op_modes[...],
        block_e,
        (((1,), (1,)), ((), ())),
        precision=lax.Precision.HIGHEST,
        preferred_element_type=f32,
    )
    wide = jnp.concatenate([part, jnp.zeros((40, LANES - 16), f32)], axis=1)
    tiles_t[pl.ds(gz, 1)] = wide.reshape(1, 40, LANES)
    share(tiles_t, tile_send, tile_recv)
    known_dots = [
        across(sum(fold(known[:, face(f)] * own_e[m : m + 1, face(f)]) for f in range(4)))
        for m in range(modes)
    ]
    known_row = row_of(known_dots)
    await_bytes(tiles_t.at[pl.ds(0, 7)], tile_recv)
    spread_own = jnp.minimum(lane // 8, 7)
    for u in range(5):
        rows = slice(8 * u, 8 * (u + 1))
        own_sum = tiles_t[0, rows, :] + tiles_t[1, rows, :] + tiles_t[2, rows, :] + tiles_t[3, rows, :]
        mixing[0, rows, :] = take(own_sum, spread_own)
        for f in range(4):
            mixing[1 + f, rows, :] = take(tiles_t[4 + f, rows, :], spread_own + 8)

    await_bytes(coarse.at[pl.ds(0, len(OFFSETS) - 1), pl.ds(0, modes)], coarse_recv)
    coeffs = coefficients(near_gather_end(), len(OFFSETS))
    gather_start(0, known_row - mixed_row(coeffs))
    exchange_start(0, modes_times(op_modes, coeffs))
    for f in range(4):
        out_ref[:, face(f)] = correction(coeffs, f)

    def gap(spot, tile):
        image[:, spot] = known[:, spot] - tile

    exchange_end(0, gap)

    quarter = chips // nz * LANES
    share_of = pl.ds(pl.multiple_of(gz * quarter, LANES), quarter)
    part_sc = jnp.zeros((8, quarter), f32)
    for m in range(modes):
        own_sum = jnp.zeros((8, LANES), f32)
        for f in range(4):
            heavy = own_e[:, face(f)] * weight[:, face(f)]
            own_sum = own_sum + fold(heavy * own_e[m : m + 1, face(f)])
            near_sum = across(fold(heavy * near_e[m : m + 1, face(f)]))
            part_sc = part_sc + near_sum * coarse[1 + f, m : m + 1, share_of]
        part_sc = part_sc + across(own_sum) * coarse[0, m : m + 1, share_of]
    plane_sc[:, modes:8, :] = jnp.zeros((plane_size, 8 - modes, quarter), f32)
    plane_sc[pl.ds(my_slot, 1), 0:modes] = part_sc[:modes].reshape(1, modes, quarter)
    mine = plane_sc.at[my_slot, pl.ds(0, modes)]
    for target in plane_list:
        send(mine, mine, sc_send, sc_recv, target)

    gather_wait(0)
    coeffs = coefficients(coarse_values(0), 5)
    sums = [jnp.zeros((8, LANES), f32) for _ in range(modes + 1)]
    for f in range(4):
        left = image[:, face(f)] - correction(coeffs, f)
        right = weight[:, face(f)] * left
        resid[:, face(f)] = left
        scaled[:, face(f)] = right
        for m in range(modes):
            sums[m] = sums[m] + fold(right * own_e[m : m + 1, face(f)])
        sums[modes] = sums[modes] + fold(left * right)
    gather_start(1, row_of([across(x) for x in sums]))

    product_a[...] = product(scaled)
    modes_product(op_heavy, True)

    await_bytes(chunks.at[pl.ds(0, chips - 1)], chunk_recv)
    await_bytes(plane_sc.at[pl.ds(0, plane_size - 1), pl.ds(0, modes)], sc_recv)
    wide_pick = lane // 8 * modes + jnp.minimum(lane % 8, modes - 1)
    left = [jnp.where(lane % 8 < modes, take(chunks[z], wide_pick), 0.0) for z in range(chips)]
    terms = lax.dot_general(
        jnp.concatenate(left, axis=0),
        plane_sc[...].reshape(plane_size * 8, quarter),
        (((1,), (0,)), ((), ())),
        precision=lax.Precision.HIGHEST,
        preferred_element_type=f32,
    )
    parts_out[...] = terms.reshape(chips, 8, quarter)
    parts_in[pl.ds(chip, 1)] = parts_out[pl.ds(chip, 1)]
    for k in outward(chips):
        if k:
            there = lax.rem(chip + k, chips)
            send(
                parts_out.at[there, pl.ds(0, modes)],
                parts_in.at[chip, pl.ds(0, modes)],
                parts_send,
                parts_recv,
                (there * 2 + core, gy, gz),
            )

    gather_wait(1)
    first_coeffs = coefficients(coarse_values(1), 5)
    rows = product_a[...] - modes_times(op_modes, first_coeffs)
    exchange_start(1, rows)
    product_b[...] = rows
    (resid_dot,) = dot_totals(1, (modes,))
    for f in range(4):
        direct[:, face(f)] = scaled[:, face(f)] - correction(first_coeffs, f)

    def keep(spot, tile):
        image[:, spot] = tile

    exchange_end(1, keep)

    sums = [jnp.zeros((8, LANES), f32) for _ in range(2 * modes + 2)]
    for f in range(4):
        left = image[:, face(f)]
        right = weight[:, face(f)] * left
        change[:, face(f)] = right
        for m in range(modes):
            sums[m] = sums[m] + fold(left * own_e[m : m + 1, face(f)])
            sums[modes + m] = sums[modes + m] + fold(right * own_e[m : m + 1, face(f)])
        sums[2 * modes] = sums[2 * modes] + fold(direct[:, face(f)] * left)
        sums[2 * modes + 1] = sums[2 * modes + 1] + fold(scaled[:, face(f)] * left)
    sums = [across(x) for x in sums]
    for m in range(modes):
        sums[2 * modes + 1] = sums[2 * modes + 1] - 2.0 * sums[m] * first_coeffs[0][m]
    gather_start(2, row_of(sums))
    product_c[...] = product(change)

    await_bytes(parts_in.at[pl.ds(0, chips - 1), pl.ds(0, modes)], parts_recv)
    total = parts_in[0, 0:modes]
    for z in range(1, chips):
        total = total + parts_in[z, 0:modes]
    twice[pl.ds(gz, 1), 0:modes] = total.reshape(1, modes, quarter)
    mine = twice.at[gz, pl.ds(0, modes)]
    for target in peer_list:
        send(mine, mine, twice_send, twice_recv, target)
    for f in range(4):
        facing = twice.at[4 * (1 + f + 1 - 2 * (f % 2)) + gz, pl.ds(0, modes)]
        for k in range(nz):
            send(mine, facing, twice_send, twice_recv, near(f, k))

    await_bytes(twice.at[pl.ds(0, 4 * 5 - 1), pl.ds(0, modes)], twice_recv)

    gather_wait(2)
    curvature, cross = dot_totals(2, (2 * modes, 2 * modes + 1))
    step = resid_dot / curvature
    values = coarse_values(2)
    image_coeffs = coefficients(values, 5)
    less = [
        [
            across(
                sum(
                    fold(
                        values[:, q * quarter : (q + 1) * quarter] * twice[4 * u + q, m : m + 1, :]
                    )
                    for q in range(nz)
                )
            )
            for m in range(modes)
        ]
        for u in range(5)
    ]
    more = coefficients(coarse_values(2, modes), 5)
    coeffs = [
        [first_coeffs[u][m] - step * (more[u][m] - less[u][m]) for m in range(modes)]
        for u in range(5)
    ]
    square = jnp.zeros((8, LANES), f32)
    for f in range(4):
        left = image[:, face(f)] - correction(image_coeffs, f)
        right = weight[:, face(f)] * left
        square = square + fold(left * right)
        second[:, face(f)] = scaled[:, face(f)] - step * right - correction(coeffs, f)
    square = across(square)
    rows = product_c[...] - modes_times(op_heavy, image_coeffs)
    rows = product_a[...] - step * rows - modes_times(op_modes, coeffs)
    alone = across(fold(second[:, block] * rows))
    mixed = across(fold(second[:, block] * product_b[...] + direct[:, block] * rows))
    peers[pl.ds(gz, 1), :] = row_of([None] * modes + [2.0 * alone, 2.0 * mixed])
    mine = peers.at[pl.ds(gz, 1)]
    for target in peer_list:
        send(mine, mine, peer_send, peer_recv, target)
    await_bytes(peers.at[pl.ds(0, nz - 1)], peer_recv)
    row = jnp.sum(peers[...], axis=0, keepdims=True) + row_of([None] * (modes + 2) + [square])
    gather_start(3, row)
    for f in range(4):
        out_ref[:, face(f)] = out_ref[:, face(f)] + step * direct[:, face(f)]
    gather_wait(3)
    alone, mixed, square = dot_totals(3, (modes, modes + 1, modes + 2))
    next_dot = resid_dot - 2.0 * step * cross + step * step * square
    ratio = next_dot / resid_dot
    step = next_dot / (alone + ratio * mixed + ratio * ratio * curvature)
    for f in range(4):
        direction = second[:, face(f)] + ratio * direct[:, face(f)]
        out_ref[:, face(f)] = out_ref[:, face(f)] + step * direction

    await_bytes(faces_out, faces_send)
    await_bytes(coarse.at[pl.ds(0, len(OFFSETS) - 1), pl.ds(0, modes)], coarse_send)
    await_bytes(plane.at[pl.ds(0, plane_size - 1)], plane_send)
    await_bytes(column.at[:, pl.ds(0, (chips - 1) * LANES)], column_send)
    await_bytes(peers.at[pl.ds(0, nz - 1)], peer_send)
    await_bytes(tiles_t.at[pl.ds(0, 7)], tile_send)
    for g in range(GATHERS):
        await_bytes(everyone.at[g, pl.ds(0, nx * ny - 1)], all_send.at[g])
    await_bytes(chunks.at[pl.ds(0, chips - 1)], chunk_send)
    await_bytes(plane_sc.at[pl.ds(0, plane_size - 1), pl.ds(0, modes)], sc_send)
    await_bytes(parts_in.at[pl.ds(0, chips - 1), pl.ds(0, modes)], parts_send)
    await_bytes(twice.at[pl.ds(0, 4 * 5 - 1), pl.ds(0, modes)], twice_send)
    for e in range(PRODUCTS):
        await_bytes(blocks.at[e, pl.ds(0, 7)], block_send.at[e])


def solution(mesh):
    sizes = tuple(mesh.shape[axis] for axis in ("gx", "gy", "gz"))
    chips, plane_size = sizes[0] // 2, 2 * sizes[1]

    def shards(
        operator,
        rhs_parts,
        stiffness,
        traces,
        coarse_inverse,
        rigid_loads,
        face_lengths,
        face_order,
        mode_count,
    ):
        rows, order = operator.shape[2:]
        load_count = rhs_parts.shape[2]
        modes = traces.shape[2]
        cap = face_order.shape[3]
        padded = chips * LANES
        quarter = padded // sizes[2]
        f32, i32 = jnp.float32, jnp.int32
        anywhere = pl.BlockSpec(memory_space=pl.ANY)
        vector = pltpu.VMEM((load_count, order), f32)
        block = pltpu.VMEM((load_count, cap), f32)
        dma = pltpu.SemaphoreType.DMA

        def by_row(array):
            return jnp.transpose(array[0], (1, 0, 2))

        result = pl.pallas_call(
            functools.partial(kernel, sizes),
            out_shape=jax.ShapeDtypeStruct((load_count, order), f32),
            in_specs=[anywhere] * 9,
            out_specs=pl.BlockSpec(memory_space=pltpu.VMEM),
            scratch_shapes=[
                pltpu.VMEM((rows, order), jnp.bfloat16),
                pltpu.VMEM((4, 16, cap), f32),
                pltpu.VMEM((4, 16, cap), f32),
                pltpu.VMEM((8, coarse_inverse.shape[3]), f32),
                pltpu.VMEM((modes, 1, load_count), f32),
                pltpu.VMEM((8, LANES), f32),
                pltpu.SMEM((1, 4), i32),
                pltpu.VMEM((4, cap), i32),
                pltpu.SMEM((1, 1), i32),
                pltpu.VMEM((len(OFFSETS), 8, padded), f32),
                pltpu.VMEM((plane_size, LANES), f32),
                pltpu.VMEM((8, padded), f32),
                pltpu.VMEM((GATHERS, sizes[0] * sizes[1], LANES), f32),
                pltpu.VMEM((sizes[2], LANES), f32),
                pltpu.VMEM((8, 40, LANES), f32),
                pltpu.VMEM((5, 40, LANES), f32),
                pltpu.VMEM((PRODUCTS, 8, 16, cap // 2), jnp.bfloat16),
                pltpu.VMEM((40, cap), f32),
                pltpu.VMEM((40, cap), f32),
                pltpu.VMEM((chips, 8, LANES), f32),
                pltpu.VMEM((plane_size, 8, quarter), f32),
                pltpu.VMEM((chips, 8, quarter), f32),
                pltpu.VMEM((chips, 8, quarter), f32),
                pltpu.VMEM((20, 8, quarter), f32),
                pltpu.VMEM((8, order), i32),
                pltpu.VMEM((8, order), i32),
            ]
            + [vector] * 10
            + [block] * 3
            + [dma, dma((7,))]
            + [dma] * 8
            + [dma((GATHERS,))] * 2
            + [dma] * 4
            + [dma((PRODUCTS,))] * 2
            + [dma] * 8,
            compiler_params=pltpu.CompilerParams(
                collective_id=0, has_side_effects=True, vmem_limit_bytes=60 << 20
            ),
        )(
            operator[0, 0],
            rhs_parts[0, 0],
            stiffness[0],
            by_row(traces),
            by_row(coarse_inverse),
            by_row(rigid_loads),
            face_lengths[0],
            face_order[0, 0],
            mode_count,
        )
        return result[None, None]

    in_specs = (
        P("gx", "gy", "gz", None),
        P("gx", "gy", None, None),
        P("gx", "gy", None),
        P("gx", "gy", None, None),
        P("gx", "gy", None, None),
        P("gx", "gy", None, None),
        P("gx", "gy", None),
        P("gx", "gy", None, None),
        P("gx", "gy"),
    )
    out_specs = P("gx", "gy", None, None)
    return jax.shard_map(shards, mesh=mesh, in_specs=in_specs, out_specs=out_specs, check_vma=False)
```

```python
import functools

import jax
import jax.numpy as jnp
from jax import lax
from jax.experimental import pallas as pl
from jax.experimental.pallas import tpu as pltpu
from jax.sharding import PartitionSpec as P

MESH = pl.DeviceIdType.MESH
GATHERS = 4
PRODUCTS = 2
LANES = 128
STEPS = ((0, 0), (-1, 0), (1, 0), (0, -1), (0, 1))
OFFSETS = STEPS + ((-2, 0), (2, 0), (0, -2), (0, 2), (-1, -1), (-1, 1), (1, -1), (1, 1))


def kernel(
    sizes,
    op_ref,
    rhs_ref,
    stiff_ref,
    traces_ref,
    inverse_ref,
    loads_ref,
    lengths_ref,
    order_ref,
    count_ref,
    out_ref,
    op_v,
    faces_out,
    faces_in,
    rows_pad,
    loads_in,
    loads_pad,
    lengths,
    order_v,
    counts,
    coarse,
    plane,
    column,
    everyone,
    tiles_t,
    mixing,
    blocks,
    all_modes,
    all_heavy,
    chunks,
    plane_sc,
    parts_out,
    parts_in,
    twice,
    lo_ref,
    hi_ref,
    own_e,
    near_e,
    weight,
    known,
    image,
    resid,
    scaled,
    direct,
    second,
    change,
    all_a,
    all_b,
    all_c,
    op_sem,
    in_sem,
    faces_send,
    faces_recv,
    coarse_send,
    coarse_recv,
    plane_send,
    plane_recv,
    column_send,
    column_recv,
    all_send,
    all_recv,
    full_send,
    full_recv,
    tile_send,
    tile_recv,
    block_send,
    block_recv,
    chunk_send,
    chunk_recv,
    sc_send,
    sc_recv,
    parts_send,
    parts_recv,
    twice_send,
    twice_recv,
):
    nx, ny, nz = sizes
    cap = order_ref.shape[1]
    order = rhs_ref.shape[1]
    tiles = cap // LANES
    modes = traces_ref.shape[0]
    chips = nx // 2
    plane_size = 2 * ny
    spread = plane_size * modes
    gx, gy, gz = lax.axis_index("gx"), lax.axis_index("gy"), lax.axis_index("gz")
    chip, core = gx // 2, gx % 2
    f32 = jnp.float32

    def near(face, z):
        sign = 2 * (face % 2) - 1
        along_x = 1 - face // 2
        return (
            lax.rem(gx + along_x * sign + nx, nx),
            lax.rem(gy + (1 - along_x) * sign + ny, ny),
            z,
        )

    def opposite(face):
        return face + 1 - 2 * (face % 2)

    def shifted(dx, dy):
        return (lax.rem(gx + dx + nx, nx), lax.rem(gy + dy + ny, ny), gz)

    def outward(count):
        return [count // 2 + ((j + 1) // 2) * (1 - 2 * (j % 2)) for j in range(count)]

    peer_list = [(gx, gy, lax.rem(gz + k, nz)) for k in (2, 1, 3)]
    plane_list = [
        (chip * 2 + lax.rem(core + 1 - c, 2), lax.rem(gy + k, ny), gz)
        for k in outward(ny)
        for c in range(2)
        if (c == 0) or k
    ]
    column_list = [(lax.rem(gx + 2 * k, nx), gy, gz) for k in outward(chips) if k]
    product_list = [near(gz, k) for k in range(nz)]
    source_list = [near(f, opposite(f)) for f in range(4)]

    op_copy = pltpu.make_async_copy(op_ref, op_v, op_sem)

    def face(f):
        return slice(f * cap, (f + 1) * cap)

    def fetch(src, dst, sem):
        pltpu.make_async_copy(src, dst, sem).start()

    op_modes, op_heavy = all_modes.at[gz], all_heavy.at[gz]

    barrier = pltpu.get_barrier_semaphore()
    greeted = (
        [shifted(dx, dy) for dx, dy in OFFSETS[1:]] + peer_list + plane_list + column_list + source_list
    )
    for target in greeted:
        pl.semaphore_signal(barrier, inc=1, device_id=target, device_id_type=MESH)

    fetch(loads_ref, loads_in, in_sem.at[0])
    fetch(count_ref, counts, in_sem.at[1])
    fetch(lengths_ref, lengths, in_sem.at[2])
    fetch(order_ref, order_v, in_sem.at[3])
    for f in range(4):
        spot = pl.ds(f * cap, cap)
        for m in range(modes):
            fetch(traces_ref.at[m, :, spot], faces_out.at[f, pl.ds(m, 1)], in_sem.at[4])
        fetch(stiff_ref.at[:, spot], faces_out.at[f, pl.ds(modes, 1)], in_sem.at[4])
        fetch(rhs_ref.at[:, spot], faces_out.at[f, pl.ds(8, 8)], in_sem.at[5])
    for m in range(modes):
        fetch(inverse_ref.at[m], rows_pad.at[pl.ds(m, 1)], in_sem.at[6])
    op_copy.start()

    sub = lax.broadcasted_iota(jnp.int32, (8, LANES), 0)
    lane = lax.broadcasted_iota(jnp.int32, (8, LANES), 1)

    def send(src, dst, send_sem, recv_sem, target):
        pltpu.make_async_remote_copy(
            src_ref=src,
            dst_ref=dst,
            send_sem=send_sem,
            recv_sem=recv_sem,
            device_id=target,
            device_id_type=MESH,
        ).start()

    def await_bytes(ref, sem):
        pltpu.make_async_copy(ref, ref, sem).wait()

    def share(ref, send_sem, recv_sem):
        mine, facing = ref.at[pl.ds(gz, 1)], ref.at[pl.ds(4 + opposite(gz), 1)]
        for target in product_list:
            send(mine, facing, send_sem, recv_sem, target)
        for target in peer_list:
            send(mine, mine, send_sem, recv_sem, target)

    def to_peers(n, ref):
        mine = ref.at[pl.ds(gz, 1)]
        for target in peer_list:
            send(mine, mine, full_send.at[n], full_recv.at[n], target)

    def from_peers(n, ref):
        await_bytes(ref.at[pl.ds(0, nz - 1)], full_recv.at[n])

    def take(values, index):
        return jnp.take_along_axis(values, index, axis=1, mode="promise_in_bounds")

    def fold(x):
        total = x[:, :LANES]
        for c in range(1, x.shape[1] // LANES):
            total = total + x[:, c * LANES : (c + 1) * LANES]
        return total

    def across(x):
        return jnp.sum(x, axis=1, keepdims=True)

    def row_of(columns):
        total = jnp.zeros((8, LANES), f32)
        for j, value in enumerate(columns):
            if value is None:
                continue
            total = total + jnp.where(lane == 8 * j + sub, value, 0.0)
        return jnp.sum(total, axis=0, keepdims=True)

    pick = jnp.minimum(8 * (lane % modes) + sub, LANES - 1)
    my_slot = core * ny + gy

    def tile_of_rows(rows, first=0):
        at = jnp.minimum(pick + 8 * first, LANES - 1)
        tile = take(jnp.broadcast_to(rows(0), (8, LANES)), at)
        for s in range(1, plane_size):
            found = take(jnp.broadcast_to(rows(s), (8, LANES)), at)
            tile = jnp.where(lane >= s * modes, found, tile)
        return tile

    def near_gather(row):
        plane[pl.ds(my_slot, 1), :] = row
        mine = plane.at[pl.ds(my_slot, 1)]
        for target in plane_list:
            send(mine, mine, plane_send, plane_recv, target)

    def near_gather_on():
        await_bytes(plane.at[pl.ds(0, plane_size - 1)], plane_recv)
        spot = pl.ds(pl.multiple_of(chip * LANES, LANES), LANES)
        column[:, spot] = tile_of_rows(lambda s: plane[s : s + 1, :])
        mine = column.at[:, spot]
        for target in column_list:
            send(mine, mine, column_send, column_recv, target)

    def near_gather_end():
        await_bytes(column.at[:, pl.ds(0, (chips - 1) * LANES)], column_recv)
        return column[...]

    pair = 2 * (chip * ny + gy)

    def gather_start(g, row):
        everyone[g, pl.ds(pair + core, 1), :] = row
        mine = everyone.at[g, pl.ds(pair + core, 1)]

        def one_plane(i, carry):
            away = chips // 2 + ((i + 1) // 2) * (1 - 2 * (i % 2))
            there = lax.rem(chip + away, chips)
            for k in outward(ny):
                for c in (1, 0):
                    target = (there * 2 + lax.rem(core + c, 2), lax.rem(gy + k, ny), gz)
                    send(mine, mine, all_send.at[g], all_recv.at[g], target)
            return carry

        lax.fori_loop(0, chips - 1, one_plane, 0)
        for target in plane_list:
            send(mine, mine, all_send.at[g], all_recv.at[g], target)

    def gather_wait(g):
        await_bytes(everyone.at[g, pl.ds(0, nx * ny - 1)], all_recv.at[g])

    def coarse_values(g, first=0):
        planes = []
        for z in range(chips):
            at = z * plane_size
            planes.append(
                tile_of_rows(
                    lambda s: everyone[g, pl.ds(at + 2 * (s % ny) + s // ny, 1), :], first
                )
            )
        return jnp.concatenate(planes, axis=1)

    def dot_totals(g, wanted):
        total = everyone[g, 0:8, :]
        for c in range(1, nx * ny // 8):
            total = total + everyone[g, 8 * c : 8 * (c + 1), :]
        total = jnp.broadcast_to(jnp.sum(total, axis=0, keepdims=True), (8, LANES))
        return [across(jnp.where(lane == 8 * j + sub, total, 0.0)) for j in wanted]

    def coefficients(values, count):
        return [
            [across(fold(values * coarse[u, m : m + 1, :])) for m in range(modes)]
            for u in range(count)
        ]

    def correction(coeffs, f):
        total = coeffs[0][0] * own_e[0:1, face(f)]
        total = total + coeffs[1 + f][0] * near_e[0:1, face(f)]
        for m in range(1, modes):
            total = total + coeffs[0][m] * own_e[m : m + 1, face(f)]
            total = total + coeffs[1 + f][m] * near_e[m : m + 1, face(f)]
        return total

    def modes_times(ref, coeffs):
        total = coeffs[0][0] * ref[0:1, :]
        for u in range(5):
            for m in range(modes):
                if u or m:
                    total = total + coeffs[u][m] * ref[8 * u + m : 8 * u + m + 1, :]
        return total

    where_of = {offset: u for u, offset in enumerate(OFFSETS)}
    own_lane = (lane % 8 == sub) & (lane < 8 * modes)

    def mixed_row(coeffs):
        total = jnp.zeros((8, LANES), f32)
        for t, at in enumerate(STEPS):
            for u, step in enumerate(STEPS):
                found = coeffs[where_of[(at[0] + step[0], at[1] + step[1])]]
                for m in range(modes):
                    total = total + found[m] * mixing[t, 8 * u + m : 8 * u + m + 1, :]
        return jnp.sum(jnp.where(own_lane, total, 0.0), axis=0, keepdims=True)

    def partner_tiles(load, start):
        given = [load(c) for c in range(tiles)]
        for b in range(tiles):
            spot = pl.ds(pl.multiple_of(start + b * LANES, LANES), LANES)
            low, high = lo_ref[:, spot], hi_ref[:, spot]
            result = take(given[0], low)
            for c in range(1, tiles):
                result = jnp.where(high == c, take(given[c], low), result)
            yield b, spot, result

    def split(x):
        high = x.astype(jnp.bfloat16)
        low = (x - high.astype(f32)).astype(jnp.bfloat16)
        return jnp.concatenate([high.astype(f32), low.astype(f32)], axis=0).astype(jnp.bfloat16)

    def times(left, columns):
        return lax.dot_general(
            left, op_v[:, columns], (((1,), (1,)), ((), ())), preferred_element_type=f32
        )

    def product(vector):
        total = jnp.zeros((8, cap), f32)
        for f in range(4):
            both = times(split(vector[:, face(f)]), face(f))
            total = total + both[:8] + both[8:]
        return total

    def exchange_start(e, rows):
        packed = jnp.concatenate([rows[:, : cap // 2], rows[:, cap // 2 :]], axis=0)
        blocks[e, pl.ds(gz, 1)] = packed.astype(jnp.bfloat16).reshape(1, 16, cap // 2)
        share(blocks.at[e], block_send.at[e], block_recv.at[e])

    def exchange_end(e, use):
        await_bytes(blocks.at[e, pl.ds(0, 7)], block_recv.at[e])

        def assemble(f, carry):
            start = pl.multiple_of(f * cap, cap)
            length = lengths[0, f]

            def tile_of(slot, c):
                row, at = 8 * (c // (tiles // 2)), c % (tiles // 2) * LANES
                both = blocks[e, slot, :, at : at + LANES].astype(f32)
                return both[row : row + 8]

            for b, spot, other in partner_tiles(lambda c: tile_of(4 + f, c), start):
                live = lane + b * LANES < length
                use(spot, jnp.where(live, tile_of(f, b) + other, 0.0))
            return carry

        lax.fori_loop(0, 4, assemble, 0)

    await_bytes(loads_in, in_sem.at[0])
    await_bytes(counts, in_sem.at[1])
    count = counts[0, 0]
    loads_pad[...] = jnp.zeros_like(loads_pad)
    for m in range(modes):
        loads_pad[m : m + 1, 0 : loads_ref.shape[2]] = loads_in[m]
    loads_tile = jnp.where(sub < count, loads_pad[...], 0.0)
    first = jnp.zeros((8, LANES), f32)
    for m in range(modes):
        only = jnp.where(sub == m, loads_tile, 0.0)
        first = first + (only if m == 0 else pltpu.roll(only, 8 * m, axis=1))
    first = jnp.sum(first, axis=0, keepdims=True)

    await_bytes(faces_out.at[:, pl.ds(0, modes + 1)], in_sem.at[4])
    await_bytes(faces_out.at[:, pl.ds(8, 8)], in_sem.at[5])
    live_mode = lax.broadcasted_iota(jnp.int32, (modes, cap), 0) < count
    for f in range(4):
        faces_out[f, 0:modes, :] = jnp.where(live_mode, faces_out[f, 0:modes, :], 0.0)
        faces_out[f, modes + 1 : 8, :] = jnp.zeros((7 - modes, cap), f32)

    pl.semaphore_wait(barrier, len(greeted))

    near_gather(first)
    for f in range(4):
        send(
            faces_out.at[f], faces_in.at[f + 1 - 2 * (f % 2)], faces_send, faces_recv, near(f, gz)
        )

    await_bytes(rows_pad.at[pl.ds(0, modes)], in_sem.at[6])
    rows_pad[modes:8, :] = jnp.zeros((8 - modes, rows_pad.shape[1]), f32)
    for z in range(chips):
        start = z * spread
        base, shift = start // LANES, start % LANES
        chunk = rows_pad[:, base * LANES : (base + 1) * LANES]
        if shift:
            chunk = pltpu.roll(chunk, LANES - shift, axis=1)
            if LANES - shift < spread:
                after = rows_pad[:, (base + 1) * LANES : (base + 2) * LANES]
                after = pltpu.roll(after, LANES - shift, axis=1)
                chunk = jnp.where(lane < LANES - shift, chunk, after)
        coarse[0, :, z * LANES : (z + 1) * LANES] = jnp.where(lane < spread, chunk, 0.0)
    for u in range(1, len(OFFSETS)):
        dx, dy = OFFSETS[u]
        send(
            coarse.at[0, pl.ds(0, modes)],
            coarse.at[u, pl.ds(0, modes)],
            coarse_send,
            coarse_recv,
            shifted(-dx, -dy),
        )

    chunks[pl.ds(chip, 1)] = coarse[
        0, :, pl.ds(pl.multiple_of(chip * LANES, LANES), LANES)
    ].reshape(1, 8, LANES)
    for k in outward(chips):
        if k:
            there = lax.rem(chip + k, chips)
            send(
                coarse.at[0, :, pl.ds(pl.multiple_of(there * LANES, LANES), LANES)],
                chunks.at[chip],
                chunk_send,
                chunk_recv,
                (there * 2 + core, gy, gz),
            )
    await_bytes(lengths, in_sem.at[2])
    await_bytes(order_v, in_sem.at[3])
    for f in range(4):
        index = jnp.broadcast_to(order_v[f : f + 1, :], (8, cap))
        lo_ref[:, face(f)] = index & (LANES - 1)
        hi_ref[:, face(f)] = index >> 7

    await_bytes(faces_in, faces_recv)

    def setup_face(f, carry):
        start = pl.multiple_of(f * cap, cap)
        length = lengths[0, f]
        for b, spot, other in partner_tiles(
            lambda c: faces_in[f, 0:8, c * LANES : (c + 1) * LANES], start
        ):
            part = slice(b * LANES, (b + 1) * LANES)
            live = lane + b * LANES < length
            mine = faces_out[f, 0:8, part]
            own_e[:, spot] = jnp.where(live & (sub < modes), mine, 0.0)
            near_e[:, spot] = jnp.where(live & (sub < modes), other, 0.0)
            stiff = jnp.broadcast_to((mine + other)[modes : modes + 1, :], (8, LANES))
            weight[:, spot] = jnp.where(live, 1.0 / jnp.where(live, stiff, 1.0), 0.0)
        for b, spot, other in partner_tiles(
            lambda c: faces_in[f, 8:16, c * LANES : (c + 1) * LANES], start
        ):
            part = slice(b * LANES, (b + 1) * LANES)
            live = lane + b * LANES < length
            known[:, spot] = jnp.where(live, faces_out[f, 8:16, part] + other, 0.0)
        return carry

    lax.fori_loop(0, 4, setup_face, 0)
    near_gather_on()

    def modes_product(ref, heavy):
        own_rows = jnp.zeros((8, cap), f32)
        for f in range(4):
            both = [own_e[:, face(f)], near_e[:, face(f)]]
            if heavy:
                both = [weight[:, face(f)] * e for e in both]
            both = times(split(jnp.concatenate(both, axis=0)), face(f))
            both = both[:16] + both[16:]
            own_rows = own_rows + both[:8]
            ref[8 * (1 + f) : 8 * (2 + f), :] = both[8:]
        ref[0:8, :] = own_rows

    op_copy.wait()
    modes_product(op_modes, False)

    block = pl.ds(pl.multiple_of(gz * cap, cap), cap)
    block_e = jnp.concatenate([own_e[:, block], near_e[:, block]], axis=0)
    part = lax.dot_general(
        op_modes[...],
        block_e,
        (((1,), (1,)), ((), ())),
        precision=lax.Precision.HIGHEST,
        preferred_element_type=f32,
    )
    wide = jnp.concatenate([part, jnp.zeros((40, LANES - 16), f32)], axis=1)
    tiles_t[pl.ds(gz, 1)] = wide.reshape(1, 40, LANES)
    share(tiles_t, tile_send, tile_recv)
    known_dots = [
        across(sum(fold(known[:, face(f)] * own_e[m : m + 1, face(f)]) for f in range(4)))
        for m in range(modes)
    ]
    known_row = row_of(known_dots)
    await_bytes(tiles_t.at[pl.ds(0, 7)], tile_recv)
    spread_own = jnp.minimum(lane // 8, 7)
    for u in range(5):
        rows = slice(8 * u, 8 * (u + 1))
        own_sum = tiles_t[0, rows, :] + tiles_t[1, rows, :] + tiles_t[2, rows, :] + tiles_t[3, rows, :]
        mixing[0, rows, :] = take(own_sum, spread_own)
        for f in range(4):
            mixing[1 + f, rows, :] = take(tiles_t[4 + f, rows, :], spread_own + 8)

    await_bytes(coarse.at[pl.ds(0, len(OFFSETS) - 1), pl.ds(0, modes)], coarse_recv)
    coeffs = coefficients(near_gather_end(), len(OFFSETS))
    gather_start(0, known_row - mixed_row(coeffs))
    exchange_start(0, modes_times(op_modes, coeffs))
    for f in range(4):
        out_ref[:, face(f)] = correction(coeffs, f)

    def gap(spot, tile):
        image[:, spot] = known[:, spot] - tile

    exchange_end(0, gap)
    to_peers(0, all_modes)

    quarter = chips // nz * LANES
    share_of = pl.ds(pl.multiple_of(gz * quarter, LANES), quarter)
    part_sc = jnp.zeros((8, quarter), f32)
    for m in range(modes):
        own_sum = jnp.zeros((8, LANES), f32)
        for f in range(4):
            heavy = own_e[:, face(f)] * weight[:, face(f)]
            own_sum = own_sum + fold(heavy * own_e[m : m + 1, face(f)])
            near_sum = across(fold(heavy * near_e[m : m + 1, face(f)]))
            part_sc = part_sc + near_sum * coarse[1 + f, m : m + 1, share_of]
        part_sc = part_sc + across(own_sum) * coarse[0, m : m + 1, share_of]
    plane_sc[:, modes:8, :] = jnp.zeros((plane_size, 8 - modes, quarter), f32)
    plane_sc[pl.ds(my_slot, 1), 0:modes] = part_sc[:modes].reshape(1, modes, quarter)
    mine = plane_sc.at[my_slot, pl.ds(0, modes)]
    for target in plane_list:
        send(mine, mine, sc_send, sc_recv, target)

    gather_wait(0)
    coeffs = coefficients(coarse_values(0), 5)
    sums = [jnp.zeros((8, LANES), f32) for _ in range(modes + 1)]
    for f in range(4):
        left = image[:, face(f)] - correction(coeffs, f)
        right = weight[:, face(f)] * left
        resid[:, face(f)] = left
        scaled[:, face(f)] = right
        for m in range(modes):
            sums[m] = sums[m] + fold(right * own_e[m : m + 1, face(f)])
        sums[modes] = sums[modes] + fold(left * right)
    gather_start(1, row_of([across(x) for x in sums]))

    all_a[pl.ds(gz, 1)] = product(scaled).reshape(1, 8, cap)
    to_peers(1, all_a)
    modes_product(op_heavy, True)
    to_peers(2, all_heavy)

    await_bytes(chunks.at[pl.ds(0, chips - 1)], chunk_recv)
    await_bytes(plane_sc.at[pl.ds(0, plane_size - 1), pl.ds(0, modes)], sc_recv)
    wide_pick = lane // 8 * modes + jnp.minimum(lane % 8, modes - 1)
    left = [jnp.where(lane % 8 < modes, take(chunks[z], wide_pick), 0.0) for z in range(chips)]
    terms = lax.dot_general(
        jnp.concatenate(left, axis=0),
        plane_sc[...].reshape(plane_size * 8, quarter),
        (((1,), (0,)), ((), ())),
        precision=lax.Precision.HIGHEST,
        preferred_element_type=f32,
    )
    parts_out[...] = terms.reshape(chips, 8, quarter)
    parts_in[pl.ds(chip, 1)] = parts_out[pl.ds(chip, 1)]
    for k in outward(chips):
        if k:
            there = lax.rem(chip + k, chips)
            send(
                parts_out.at[there, pl.ds(0, modes)],
                parts_in.at[chip, pl.ds(0, modes)],
                parts_send,
                parts_recv,
                (there * 2 + core, gy, gz),
            )

    gather_wait(1)
    first_coeffs = coefficients(coarse_values(1), 5)
    exchange_start(1, all_a[gz] - modes_times(op_modes, first_coeffs))
    (resid_dot,) = dot_totals(1, (modes,))
    for f in range(4):
        direct[:, face(f)] = scaled[:, face(f)] - correction(first_coeffs, f)

    def keep(spot, tile):
        image[:, spot] = tile

    exchange_end(1, keep)

    sums = [jnp.zeros((8, LANES), f32) for _ in range(2 * modes + 2)]
    for f in range(4):
        left = image[:, face(f)]
        right = weight[:, face(f)] * left
        change[:, face(f)] = right
        for m in range(modes):
            sums[m] = sums[m] + fold(left * own_e[m : m + 1, face(f)])
            sums[modes + m] = sums[modes + m] + fold(right * own_e[m : m + 1, face(f)])
        sums[2 * modes] = sums[2 * modes] + fold(direct[:, face(f)] * left)
        sums[2 * modes + 1] = sums[2 * modes + 1] + fold(scaled[:, face(f)] * left)
    sums = [across(x) for x in sums]
    for m in range(modes):
        sums[2 * modes + 1] = sums[2 * modes + 1] - 2.0 * sums[m] * first_coeffs[0][m]
    gather_start(2, row_of(sums))
    all_c[pl.ds(gz, 1)] = product(change).reshape(1, 8, cap)
    to_peers(3, all_c)

    await_bytes(parts_in.at[pl.ds(0, chips - 1), pl.ds(0, modes)], parts_recv)
    total = parts_in[0, 0:modes]
    for z in range(1, chips):
        total = total + parts_in[z, 0:modes]
    twice[pl.ds(gz, 1), 0:modes] = total.reshape(1, modes, quarter)
    mine = twice.at[gz, pl.ds(0, modes)]
    for target in peer_list:
        send(mine, mine, twice_send, twice_recv, target)
    for f in range(4):
        facing = twice.at[4 * (1 + f + 1 - 2 * (f % 2)) + gz, pl.ds(0, modes)]
        for k in range(nz):
            send(mine, facing, twice_send, twice_recv, near(f, k))

    from_peers(0, all_modes)
    from_peers(1, all_a)
    for k in range(nz):
        all_b[k] = all_a[k] - modes_times(all_modes.at[k], first_coeffs)
    from_peers(2, all_heavy)
    from_peers(3, all_c)
    await_bytes(twice.at[pl.ds(0, 4 * 5 - 1), pl.ds(0, modes)], twice_recv)

    gather_wait(2)
    curvature, cross = dot_totals(2, (2 * modes, 2 * modes + 1))
    step = resid_dot / curvature
    values = coarse_values(2)
    image_coeffs = coefficients(values, 5)
    less = [
        [
            across(
                sum(
                    fold(
                        values[:, q * quarter : (q + 1) * quarter] * twice[4 * u + q, m : m + 1, :]
                    )
                    for q in range(nz)
                )
            )
            for m in range(modes)
        ]
        for u in range(5)
    ]
    more = coefficients(coarse_values(2, modes), 5)
    coeffs = [
        [first_coeffs[u][m] - step * (more[u][m] - less[u][m]) for m in range(modes)]
        for u in range(5)
    ]
    square = jnp.zeros((8, LANES), f32)
    for f in range(4):
        left = image[:, face(f)] - correction(image_coeffs, f)
        right = weight[:, face(f)] * left
        square = square + fold(left * right)
        second[:, face(f)] = scaled[:, face(f)] - step * right - correction(coeffs, f)
    square = across(square)
    alone = mixed = jnp.zeros((8, LANES), f32)
    for k in range(nz):
        rows = all_c[k] - modes_times(all_heavy.at[k], image_coeffs)
        rows = all_a[k] - step * rows - modes_times(all_modes.at[k], coeffs)
        alone = alone + fold(second[:, face(k)] * rows)
        mixed = mixed + fold(second[:, face(k)] * all_b[k] + direct[:, face(k)] * rows)
    row = row_of([None] * modes + [2.0 * across(alone), 2.0 * across(mixed), square])
    gather_start(3, row)
    for f in range(4):
        out_ref[:, face(f)] = out_ref[:, face(f)] + step * direct[:, face(f)]
    gather_wait(3)
    alone, mixed, square = dot_totals(3, (modes, modes + 1, modes + 2))
    next_dot = resid_dot - 2.0 * step * cross + step * step * square
    ratio = next_dot / resid_dot
    step = next_dot / (alone + ratio * mixed + ratio * ratio * curvature)
    for f in range(4):
        direction = second[:, face(f)] + ratio * direct[:, face(f)]
        out_ref[:, face(f)] = out_ref[:, face(f)] + step * direction

    await_bytes(faces_out, faces_send)
    await_bytes(coarse.at[pl.ds(0, len(OFFSETS) - 1), pl.ds(0, modes)], coarse_send)
    await_bytes(plane.at[pl.ds(0, plane_size - 1)], plane_send)
    await_bytes(column.at[:, pl.ds(0, (chips - 1) * LANES)], column_send)
    for n, ref in enumerate((all_modes, all_a, all_heavy, all_c)):
        await_bytes(ref.at[pl.ds(0, nz - 1)], full_send.at[n])
    await_bytes(tiles_t.at[pl.ds(0, 7)], tile_send)
    for g in range(GATHERS):
        await_bytes(everyone.at[g, pl.ds(0, nx * ny - 1)], all_send.at[g])
    await_bytes(chunks.at[pl.ds(0, chips - 1)], chunk_send)
    await_bytes(plane_sc.at[pl.ds(0, plane_size - 1), pl.ds(0, modes)], sc_send)
    await_bytes(parts_in.at[pl.ds(0, chips - 1), pl.ds(0, modes)], parts_send)
    await_bytes(twice.at[pl.ds(0, 4 * 5 - 1), pl.ds(0, modes)], twice_send)
    for e in range(PRODUCTS):
        await_bytes(blocks.at[e, pl.ds(0, 7)], block_send.at[e])


def solution(mesh):
    sizes = tuple(mesh.shape[axis] for axis in ("gx", "gy", "gz"))
    chips, plane_size = sizes[0] // 2, 2 * sizes[1]

    def shards(
        operator,
        rhs_parts,
        stiffness,
        traces,
        coarse_inverse,
        rigid_loads,
        face_lengths,
        face_order,
        mode_count,
    ):
        rows, order = operator.shape[2:]
        load_count = rhs_parts.shape[2]
        modes = traces.shape[2]
        cap = face_order.shape[3]
        padded = chips * LANES
        quarter = padded // sizes[2]
        f32, i32 = jnp.float32, jnp.int32
        anywhere = pl.BlockSpec(memory_space=pl.ANY)
        vector = pltpu.VMEM((load_count, order), f32)
        block = pltpu.VMEM((sizes[2], load_count, cap), f32)
        dma = pltpu.SemaphoreType.DMA

        def by_row(array):
            return jnp.transpose(array[0], (1, 0, 2))

        result = pl.pallas_call(
            functools.partial(kernel, sizes),
            out_shape=pltpu.VMEM((load_count, order), f32),
            in_specs=[anywhere] * 9,
            out_specs=pl.BlockSpec(memory_space=pltpu.VMEM),
            scratch_shapes=[
                pltpu.VMEM((rows, order), jnp.bfloat16),
                pltpu.VMEM((4, 16, cap), f32),
                pltpu.VMEM((4, 16, cap), f32),
                pltpu.VMEM((8, coarse_inverse.shape[3]), f32),
                pltpu.VMEM((modes, 1, load_count), f32),
                pltpu.VMEM((8, LANES), f32),
                pltpu.SMEM((1, 4), i32),
                pltpu.VMEM((4, cap), i32),
                pltpu.SMEM((1, 1), i32),
                pltpu.VMEM((len(OFFSETS), 8, padded), f32),
                pltpu.VMEM((plane_size, LANES), f32),
                pltpu.VMEM((8, padded), f32),
                pltpu.VMEM((GATHERS, sizes[0] * sizes[1], LANES), f32),
                pltpu.VMEM((8, 40, LANES), f32),
                pltpu.VMEM((5, 40, LANES), f32),
                pltpu.VMEM((PRODUCTS, 8, 16, cap // 2), jnp.bfloat16),
                pltpu.VMEM((sizes[2], 40, cap), f32),
                pltpu.VMEM((sizes[2], 40, cap), f32),
                pltpu.VMEM((chips, 8, LANES), f32),
                pltpu.VMEM((plane_size, 8, quarter), f32),
                pltpu.VMEM((chips, 8, quarter), f32),
                pltpu.VMEM((chips, 8, quarter), f32),
                pltpu.VMEM((20, 8, quarter), f32),
                pltpu.VMEM((8, order), i32),
                pltpu.VMEM((8, order), i32),
            ]
            + [vector] * 10
            + [block] * 3
            + [dma, dma((7,))]
            + [dma] * 8
            + [dma((GATHERS,))] * 2
            + [dma((4,))] * 2
            + [dma] * 2
            + [dma((PRODUCTS,))] * 2
            + [dma] * 8,
            compiler_params=pltpu.CompilerParams(
                collective_id=0, has_side_effects=True, vmem_limit_bytes=60 << 20
            ),
        )(
            operator[0, 0],
            rhs_parts[0, 0],
            stiffness[0],
            by_row(traces),
            by_row(coarse_inverse),
            by_row(rigid_loads),
            face_lengths[0],
            face_order[0, 0],
            mode_count,
        )
        return result[None, None]

    in_specs = (
        P("gx", "gy", "gz", None),
        P("gx", "gy", None, None),
        P("gx", "gy", None),
        P("gx", "gy", None, None),
        P("gx", "gy", None, None),
        P("gx", "gy", None, None),
        P("gx", "gy", None),
        P("gx", "gy", None, None),
        P("gx", "gy"),
    )
    out_specs = P("gx", "gy", None, None)
    return jax.shard_map(shards, mesh=mesh, in_specs=in_specs, out_specs=out_specs, check_vma=False)
```
